32 devices in a mesh: scene: 4 (over z), rows: 8 (over y, x, core).
Axes of the slice: x: 2, y: 2, z: 4, core: 2. Of those that a mesh axis runs over, the one named last changes fastest.
Arguments:
- observations: float32 [512, 256, 512], P(('scene', 'rows')), may hold values from -100 to 100
- inverse_factor: float32 [512, 512], replicated, may hold values from -2 to 2, as said below
- tile_count: int32 [32], P(('scene', 'rows')), may hold values from 0 to 16
- tile_owner: int32 [512], P(('scene', 'rows')), may hold values from 0 to 3, as said below
- tile_slot: int32 [512], P(('scene', 'rows')), may hold values from 0 to 7
Outputs:
- orthonormal: float32 [256, 256, 512], P(('scene', 'rows'))
- factor: float32 [512, 512], replicated
The draws below stay inside these ranges and needn't reach their ends.
Inputs may be any that keep to these rules, and one draw needn't show every extreme that they name: `tile_owner`: within each group (fixed rows index), every row-block owner's 8 slots are each named by exactly one live tile of that group; at most 4 live tiles of one device name the same owner, and in every group one device names every owner 4 times. `inverse_factor`: upper triangular with a positive diagonal.
All inputs are finite; a program needn't handle non-finite values.
Results may differ from the reference program's by a relative error of at most 0.0001.
Values sent between devices are 32-bit elements; how exact they have to be, the bound alone decides.
A program may use at most 128 MiB of HBM per device.

```python
import math
import jax
import jax.numpy as jnp
from jax import lax

NSRC = 512
TILE = 256
OWN_TILES = 8
SCENES = 4
GROUPS = 8
PAIR = 4
CAP = 16
ROWS_ALL = 65536


def plan_tiles(key):
    base_key = jax.random.fold_in(key, 7)
    heavy_key, bias_key, noise_key, order_key, list_key, dead_key = jax.random.split(base_key, 6)
    seat_count = SCENES * PAIR
    seat_index = jnp.arange(seat_count, dtype=jnp.int32)
    seat_src = seat_index // PAIR
    heavy_src = jax.random.randint(heavy_key, (GROUPS,), 0, SCENES)
    src_bias = jax.random.randint(bias_key, (GROUPS, SCENES), 0, 2 ** 18)
    seat_noise = jax.random.randint(noise_key, (GROUPS, SCENES, seat_count), 0, 2 ** 18)
    seat_score = (seat_noise + src_bias[:, None, :][:, :, seat_src]) * seat_count + seat_index
    seat_score = seat_score + jnp.where(seat_src[None, None, :] == heavy_src[:, None, None], 2 ** 28, 0)
    top_values, top_index = lax.top_k(seat_score, OWN_TILES)
    chosen = (top_index[..., None] == seat_index).any(-2)
    rank_key = jax.random.randint(order_key, (GROUPS, SCENES, seat_count), 0, 2 ** 20) * seat_count + seat_index
    smaller = chosen[:, :, None, :] & (rank_key[:, :, None, :] < rank_key[:, :, :, None])
    dest_slot = smaller.sum(-1).astype(jnp.int32)
    dead_slot = jax.random.randint(dead_key, (GROUPS, SCENES, seat_count), 0, OWN_TILES)
    dest_slot = jnp.where(chosen, dest_slot, dead_slot)
    dest_owner = jnp.broadcast_to(jnp.arange(SCENES, dtype=jnp.int32)[None, :, None], (GROUPS, SCENES, seat_count))

    def source_view(values):
        shaped = values.reshape(GROUPS, SCENES, SCENES, PAIR)
        return jnp.transpose(shaped, (2, 0, 1, 3)).reshape(SCENES, GROUPS, CAP)
    is_live = source_view(chosen.astype(jnp.int32))
    owner_view = source_view(dest_owner)
    slot_view = source_view(dest_slot)
    list_key_values = jax.random.randint(list_key, (SCENES, GROUPS, CAP), 0, 2 ** 20) * CAP + jnp.arange(CAP, dtype=jnp.int32)
    list_key_values = list_key_values + jnp.where(is_live > 0, 0, 2 ** 26)
    list_order = jnp.argsort(list_key_values, axis=-1)
    owner_list = jnp.take_along_axis(owner_view, list_order, axis=-1)
    slot_list = jnp.take_along_axis(slot_view, list_order, axis=-1)
    live_count = is_live.sum(-1).astype(jnp.int32)
    return (live_count.reshape(-1), owner_list.reshape(-1).astype(jnp.int32), slot_list.reshape(-1).astype(jnp.int32))


def draw_tile_count(key, part):
    return plan_tiles(key)[0]


def draw_tile_owner(key, part):
    return plan_tiles(key)[1]


def draw_tile_slot(key, part):
    return plan_tiles(key)[2]


def draw_observations(key, part):
    rows_total = SCENES * GROUPS * CAP
    normal_key, scale_key, column_key = jax.random.split(key, 3)
    base_values = jnp.clip(jax.random.normal(normal_key, (rows_total, TILE, NSRC), jnp.float32), -4.0, 4.0)
    row_scale = 0.3 * 10.0 ** jax.random.uniform(scale_key, (rows_total, TILE, 1), jnp.float32)
    block_id = jnp.arange(rows_total, dtype=jnp.int32) // CAP
    group_id = (block_id % GROUPS).astype(jnp.float32)
    rising = 3.0 ** (0.5 * group_id / max(GROUPS - 1, 1))
    column_scale = 10.0 ** (0.5 * jax.random.uniform(column_key, (NSRC,), jnp.float32))
    result = base_values * row_scale * rising[:, None, None] * column_scale
    return result.astype(jnp.float32)


def draw_inverse_factor(key, part):
    diag_key, off_key = jax.random.split(key)
    diagonal = 0.5 * 4.0 ** jax.random.uniform(diag_key, (NSRC,), jnp.float32)
    off_values = jnp.clip(jax.random.normal(off_key, (NSRC, NSRC), jnp.float32), -4.0, 4.0) * (0.5 / math.sqrt(NSRC))
    return (jnp.triu(off_values, 1) + jnp.diag(diagonal)).astype(jnp.float32)


def setup_inputs(seed: int = 0) -> dict:
    key_list = jax.random.split(jax.random.key(seed), 6)
    return {
        "observations": draw_observations(jax.random.fold_in(key_list[5], 71), 0),
        "inverse_factor": draw_inverse_factor(jax.random.fold_in(key_list[5], 71), 0),
        "tile_count": draw_tile_count(jax.random.fold_in(key_list[5], 71), 0),
        "tile_owner": draw_tile_owner(jax.random.fold_in(key_list[5], 71), 0),
        "tile_slot": draw_tile_slot(jax.random.fold_in(key_list[5], 71), 0),
    }


def reference(observations, inverse_factor, tile_count, tile_owner, tile_slot):
    blocks = SCENES * GROUPS
    block_id = jnp.arange(blocks, dtype=jnp.int32)
    group_id = block_id % GROUPS
    is_live = jnp.arange(CAP, dtype=jnp.int32)[None, :] < tile_count[:, None]
    dest_index = (tile_owner.reshape(blocks, CAP) * GROUPS + group_id[:, None]) * OWN_TILES + tile_slot.reshape(blocks, CAP)
    dest_index = jnp.where(is_live, dest_index, blocks * OWN_TILES).astype(jnp.int32)
    source_of = jnp.zeros((blocks * OWN_TILES + 1,), jnp.int32)
    source_of = source_of.at[dest_index.reshape(-1)].set(jnp.arange(blocks * CAP, dtype=jnp.int32))
    source_of = source_of[:blocks * OWN_TILES].reshape(blocks, OWN_TILES)

    def project(indices):
        tile_block = jnp.take(observations, indices, axis=0).reshape(-1, NSRC)
        return jnp.dot(tile_block.astype(jnp.float32), inverse_factor.astype(jnp.float32), precision=lax.Precision.HIGHEST, preferred_element_type=jnp.float32)

    def accumulate(carry, indices):
        projected = project(indices)
        term = lax.dot_general(projected.astype(jnp.float32), projected.astype(jnp.float32), (((0,), (0,)), ((), ())), precision=lax.Precision.HIGHEST, preferred_element_type=jnp.float32)
        return (carry + term, None)
    gram_sum, unused = lax.scan(accumulate, jnp.zeros((NSRC, NSRC), jnp.float32), source_of)
    weight = gram_sum / ROWS_ALL
    lower_factor = jnp.linalg.cholesky(weight)
    inv_upper = jax.scipy.linalg.solve_triangular(lower_factor, jnp.eye(NSRC, dtype=jnp.float32), lower=True).T

    def finish(indices):
        result = jnp.dot(project(indices).astype(jnp.float32), inv_upper.astype(jnp.float32), precision=lax.Precision.HIGHEST, preferred_element_type=jnp.float32)
        return result.reshape(OWN_TILES, TILE, NSRC)
    orthonormal = lax.map(finish, source_of).reshape(blocks * OWN_TILES, TILE, NSRC)
    return (orthonormal, lower_factor.T)
```

```python
import functools

import jax
import jax.numpy as jnp
from jax import lax
from jax.experimental import pallas as pl
from jax.experimental.pallas import tpu as pltpu
from jax.sharding import PartitionSpec as P

OWN_TILES = 8
NB = 128
HALF = 256


def split(x):
    hi = x.astype(jnp.bfloat16)
    return hi, (x - hi.astype(jnp.float32)).astype(jnp.bfloat16)


def mm(a, b):
    return jnp.dot(a, b, preferred_element_type=jnp.float32)


def upper_product(x, uh, ul):
    xh, xl = split(x)
    left = slice(0, HALF)
    right = slice(HALF, None)
    a = mm(xh[:, left], uh[left, left]) + (mm(xh[:, left], ul[left, left]) + mm(xl[:, left], uh[left, left]))
    b = mm(xh, uh[:, right]) + (mm(xh, ul[:, right]) + mm(xl, uh[:, right]))
    return a, b


def copy_kernel(index_ref, x_ref, o_ref):
    o_ref[...] = x_ref[...]


def gather_tiles(index, tiles):
    block = (1,) + tiles.shape[1:]
    return pl.pallas_call(
        copy_kernel,
        grid_spec=pltpu.PrefetchScalarGridSpec(
            num_scalar_prefetch=1,
            grid=(index.shape[0],),
            in_specs=[pl.BlockSpec(block, lambda i, idx: (idx[i], 0, 0))],
            out_specs=pl.BlockSpec(block, lambda i, idx: (i, 0, 0)),
        ),
        out_shape=jax.ShapeDtypeStruct((index.shape[0],) + tiles.shape[1:], tiles.dtype),
        name="gather_tiles",
    )(index, tiles)


def gram_kernel(count_ref, x_ref, r_ref, g_ref, rh, rl, low, cross):
    i = pl.program_id(0)

    @pl.when(i == 0)
    def _():
        h, l = split(r_ref[...])
        rh[...] = h
        rl[...] = l
        low[...] = jnp.zeros_like(low)
        cross[...] = jnp.zeros_like(cross)

    @pl.when(i < count_ref[0])
    def _():
        a, b = upper_product(x_ref[0], rh[...], rl[...])
        ah, al = split(a)
        bh, bl = split(b)
        at = ah.T
        bt = bh.T
        low[:HALF, :HALF] += mm(at, ah)
        low[HALF:, :HALF] += mm(bt, ah)
        low[HALF:, HALF:] += mm(bt, bh)
        cross[:HALF, :HALF] += mm(at, al)
        cross[:HALF, HALF:] += mm(at, bl)
        cross[HALF:, :HALF] += mm(bt, al)
        cross[HALF:, HALF:] += mm(bt, bl)

    @pl.when(i == pl.num_programs(0) - 1)
    def _():
        c = cross[...]
        g_ref[...] = c + c.T
        g_ref[:HALF, :HALF] += low[:HALF, :HALF]
        g_ref[HALF:, HALF:] += low[HALF:, HALF:]
        corner = low[HALF:, :HALF]
        g_ref[HALF:, :HALF] += corner
        g_ref[:HALF, HALF:] += corner.T


def local_gram(count, tiles, inverse_factor):
    capacity, rows, n = tiles.shape
    return pl.pallas_call(
        gram_kernel,
        grid_spec=pltpu.PrefetchScalarGridSpec(
            num_scalar_prefetch=1,
            grid=(capacity,),
            in_specs=[
                pl.BlockSpec(
                    (1, rows, n), lambda i, c: (jnp.minimum(i, jnp.maximum(c[0] - 1, 0)), 0, 0)
                ),
                pl.BlockSpec((n, n), lambda i, c: (0, 0)),
            ],
            out_specs=pl.BlockSpec((n, n), lambda i, c: (0, 0)),
            scratch_shapes=[
                pltpu.VMEM((n, n), jnp.bfloat16),
                pltpu.VMEM((n, n), jnp.bfloat16),
                pltpu.VMEM((n, n), jnp.float32),
                pltpu.VMEM((n, n), jnp.float32),
            ],
        ),
        out_shape=jax.ShapeDtypeStruct((n, n), jnp.float32),
        compiler_params=pltpu.CompilerParams(vmem_limit_bytes=40 * 2**20),
        cost_estimate=pl.CostEstimate(
            flops=8 * capacity * rows * n * n, bytes_accessed=4 * capacity * rows * n, transcendentals=0
        ),
        name="local_gram",
    )(count, tiles, inverse_factor)


def eliminate(block):
    lane = lax.broadcasted_iota(jnp.int32, (8, NB), 1)
    sub = lax.broadcasted_iota(jnp.int32, (8, 1), 0)
    groups = [block[8 * g : 8 * g + 8, :] for g in range(NB // 8)]
    for j in range(NB - 1):
        first, r = divmod(j, 8)
        row = groups[first][r : r + 1, :]
        inverse = 1.0 / row[:, j : j + 1]
        here = lane == j
        row = jnp.where(here[:1], 1.0, row)
        for g in range(first if r < 7 else first + 1, NB // 8):
            c = groups[g]
            coef = c[:, j : j + 1] * inverse
            if g == first:
                live = sub > r
                coef = jnp.where(live, coef, 0.0)
                base = jnp.where(here & live, 0.0, c)
            else:
                base = jnp.where(here, 0.0, c)
            groups[g] = base - coef * row
    return jnp.concatenate(groups, axis=0)


def hdot(a, b, dims=((1,), (0,))):
    return lax.dot_general(
        a, b, (dims, ((), ())), precision=lax.Precision.HIGHEST, preferred_element_type=jnp.float32
    )


def factor_kernel(rows_all, g_ref, r_ref, u_ref, mh_ref, ml_ref, work):
    n = g_ref.shape[0]
    work[:, :n] = g_ref[...] / rows_all
    work[:, n:] = (
        lax.broadcasted_iota(jnp.int32, (n, n), 0) == lax.broadcasted_iota(jnp.int32, (n, n), 1)
    ).astype(jnp.float32)

    def step(k, carry):
        at = pl.multiple_of(k * NB, NB)
        here = pl.ds(at, NB)
        done = eliminate(work[here, here])
        i = lax.broadcasted_iota(jnp.int32, (NB, NB), 0)
        j = lax.broadcasted_iota(jnp.int32, (NB, NB), 1)
        scale = lax.rsqrt(jnp.sum(jnp.where(i == j, done, 0.0), axis=1, keepdims=True))
        inverse = jnp.where(i > j, done, jnp.where(i == j, 1.0, 0.0)) * scale
        panel = hdot(inverse, work[here, :])
        work[here, :] = panel
        work[here, here] = jnp.where(i <= j, done, 0.0) * scale
        column = lax.broadcasted_iota(jnp.int32, (NB, n), 1)
        coef = jnp.where(column >= at + NB, panel[:, :n], 0.0)

        @pl.when(k < n // NB - 1)
        def _():
            work[...] -= hdot(coef, panel, ((0,), (0,)))

        return carry

    lax.fori_loop(0, n // NB, step, 0)
    i = lax.broadcasted_iota(jnp.int32, (n, n), 0)
    j = lax.broadcasted_iota(jnp.int32, (n, n), 1)
    u_ref[...] = jnp.where(i <= j, work[:, :n], 0.0)
    m = hdot(r_ref[...], work[:, n:], ((1,), (1,)))
    h, l = split(m)
    mh_ref[...] = h
    ml_ref[...] = l


def factorise(gram, inverse_factor, rows_all):
    n = gram.shape[0]
    return pl.pallas_call(
        functools.partial(factor_kernel, rows_all),
        out_shape=[
            jax.ShapeDtypeStruct((n, n), jnp.float32),
            jax.ShapeDtypeStruct((n, n), jnp.bfloat16),
            jax.ShapeDtypeStruct((n, n), jnp.bfloat16),
        ],
        in_specs=[pl.BlockSpec(memory_space=pltpu.VMEM)] * 2,
        out_specs=[pl.BlockSpec(memory_space=pltpu.VMEM)] * 3,
        scratch_shapes=[pltpu.VMEM((n, 2 * n), jnp.float32)],
        compiler_params=pltpu.CompilerParams(vmem_limit_bytes=40 * 2**20),
        cost_estimate=pl.CostEstimate(flops=40 * n**3, bytes_accessed=16 * n * n, transcendentals=0),
        name="factorise",
    )(gram, inverse_factor)


def last_kernel(index_ref, x_ref, mh_ref, ml_ref, o_ref):
    a, b = upper_product(x_ref[0], mh_ref[...], ml_ref[...])
    o_ref[0, :, :HALF] = a
    o_ref[0, :, HALF:] = b


def last_product(index, tiles, mh, ml):
    rows, n = tiles.shape[1:]
    whole = pl.BlockSpec((n, n), lambda i, idx: (0, 0))
    return pl.pallas_call(
        last_kernel,
        grid_spec=pltpu.PrefetchScalarGridSpec(
            num_scalar_prefetch=1,
            grid=(OWN_TILES,),
            in_specs=[pl.BlockSpec((1, rows, n), lambda i, idx: (idx[i], 0, 0)), whole, whole],
            out_specs=pl.BlockSpec((1, rows, n), lambda i, idx: (i, 0, 0)),
        ),
        out_shape=jax.ShapeDtypeStruct((OWN_TILES, rows, n), jnp.float32),
        compiler_params=pltpu.CompilerParams(vmem_limit_bytes=32 * 2**20),
        name="last_product",
    )(index, tiles, mh, ml)


def seats(owner, count, scenes):
    capacity = owner.shape[0]
    position = jnp.arange(capacity, dtype=jnp.int32)
    is_live = position < count
    earlier = (owner[:, None] == owner[None, :]) & is_live[None, :] & (position[None, :] < position[:, None])
    rank = earlier.astype(jnp.int32).sum(1)
    return is_live, rank


def shards(observations, inverse_factor, tile_count, tile_owner, tile_slot):
    scenes = lax.axis_size("scene")
    devices = scenes * lax.axis_size("rows")
    capacity = tile_owner.shape[0]
    pair_most = capacity // scenes
    tile_rows, n = observations.shape[1:]
    position = jnp.arange(capacity, dtype=jnp.int32)

    is_live, rank = seats(tile_owner, tile_count[0], scenes)
    target = jnp.where(is_live, tile_owner * pair_most + rank, -1)
    selector = (target[None, :] == position[:, None]).astype(jnp.int32)
    chosen = (selector * position[None, :]).sum(1)
    outgoing = gather_tiles(chosen, observations)
    received = lax.all_to_all(
        outgoing.reshape(scenes, pair_most, tile_rows, n), "scene", split_axis=0, concat_axis=0, tiled=True
    ).reshape(capacity, tile_rows, n)

    me = lax.axis_index("scene")
    note = jnp.where(is_live, (tile_owner * pair_most + rank) * OWN_TILES + tile_slot, -1)
    notes = lax.all_gather(note, "scene")
    seat = notes // OWN_TILES
    mine = (notes >= 0) & (seat // pair_most == me)
    place = jnp.arange(scenes, dtype=jnp.int32)[:, None] * pair_most + seat % pair_most
    match = mine[None] & ((notes % OWN_TILES)[None] == jnp.arange(OWN_TILES, dtype=jnp.int32)[:, None, None])
    order = jnp.where(match, place[None], 0).sum((1, 2))

    gram = lax.psum(local_gram(tile_count, observations, inverse_factor), ("scene", "rows"))
    factor, mh, ml = factorise(gram, inverse_factor, devices * OWN_TILES * tile_rows)
    return last_product(order, received, mh, ml), factor


def solution(mesh):
    in_specs = (
        P(("scene", "rows"), None, None),
        P(),
        P(("scene", "rows")),
        P(("scene", "rows")),
        P(("scene", "rows")),
    )
    out_specs = (P(("scene", "rows"), None, None), P())
    return jax.shard_map(shards, mesh=mesh, in_specs=in_specs, out_specs=out_specs, check_vma=False)
```

```python
import functools

import jax
import jax.numpy as jnp
from jax import lax
from jax.experimental import pallas as pl
from jax.experimental.pallas import tpu as pltpu
from jax.sharding import PartitionSpec as P

OWN_TILES = 8
NB = 128
HALF = 256
FIRST = 48


def split(x):
    hi = x.astype(jnp.bfloat16)
    return hi, (x - hi.astype(jnp.float32)).astype(jnp.bfloat16)


def mm(a, b):
    return jnp.dot(a, b, preferred_element_type=jnp.float32)


def upper_product(x, uh, ul):
    xh, xl = split(x)
    left = slice(0, HALF)
    right = slice(HALF, None)
    a = mm(xh[:, left], uh[left, left]) + (mm(xh[:, left], ul[left, left]) + mm(xl[:, left], uh[left, left]))
    b = mm(xh, uh[:, right]) + (mm(xh, ul[:, right]) + mm(xl, uh[:, right]))
    return a, b


def copy_kernel(index_ref, x_ref, o_ref):
    o_ref[0] = x_ref[0, x_ref.shape[1] - o_ref.shape[1] :, :]


def gather_rows(index, tiles, start, rows):
    tile_rows, n = tiles.shape[1:]
    taken = rows if start == 0 else tile_rows
    return pl.pallas_call(
        copy_kernel,
        grid_spec=pltpu.PrefetchScalarGridSpec(
            num_scalar_prefetch=1,
            grid=(index.shape[0],),
            in_specs=[pl.BlockSpec((1, taken, n), lambda i, idx: (idx[i], 0, 0))],
            out_specs=pl.BlockSpec((1, rows, n), lambda i, idx: (i, 0, 0)),
        ),
        out_shape=jax.ShapeDtypeStruct((index.shape[0], rows, n), tiles.dtype),
        name="gather_rows",
    )(index, tiles)


def lower_blocks(n):
    return [(i, j) for i in range(n // NB) for j in range(i + 1)]


def gram_kernel(count_ref, x_ref, r_ref, g_ref, rh, rl, low, cross):
    i = pl.program_id(0)

    @pl.when(i == 0)
    def _():
        h, l = split(r_ref[...])
        rh[...] = h
        rl[...] = l
        low[...] = jnp.zeros_like(low)
        cross[...] = jnp.zeros_like(cross)

    @pl.when(i < count_ref[0])
    def _():
        a, b = upper_product(x_ref[0], rh[...], rl[...])
        ah, al = split(a)
        bh, bl = split(b)
        at = ah.T
        bt = bh.T
        low[:HALF, :HALF] += mm(at, ah)
        low[HALF:, :HALF] += mm(bt, ah)
        low[HALF:, HALF:] += mm(bt, bh)
        cross[:HALF, :HALF] += mm(at, al)
        cross[:HALF, HALF:] += mm(at, bl)
        cross[HALF:, :HALF] += mm(bt, al)
        cross[HALF:, HALF:] += mm(bt, bl)

    @pl.when(i == pl.num_programs(0) - 1)
    def _():
        blocks = lower_blocks(low.shape[0])
        for k, (bi, bj) in enumerate(blocks):
            rows = slice(bi * NB, (bi + 1) * NB)
            cols = slice(bj * NB, (bj + 1) * NB)
            g_ref[k * NB : (k + 1) * NB, :] = low[rows, cols] + (cross[rows, cols] + cross[cols, rows].T)
        used = len(blocks) * NB
        if used < g_ref.shape[0]:
            g_ref[used:, :] = jnp.zeros((g_ref.shape[0] - used, NB), jnp.float32)


def local_gram(count, tiles, inverse_factor, packed):
    capacity, rows, n = tiles.shape
    return pl.pallas_call(
        gram_kernel,
        grid_spec=pltpu.PrefetchScalarGridSpec(
            num_scalar_prefetch=1,
            grid=(capacity,),
            in_specs=[
                pl.BlockSpec(
                    (1, rows, n), lambda i, c: (jnp.minimum(i, jnp.maximum(c[0] - 1, 0)), 0, 0)
                ),
                pl.BlockSpec((n, n), lambda i, c: (0, 0)),
            ],
            out_specs=pl.BlockSpec((packed, NB), lambda i, c: (0, 0)),
            scratch_shapes=[
                pltpu.VMEM((n, n), jnp.bfloat16),
                pltpu.VMEM((n, n), jnp.bfloat16),
                pltpu.VMEM((n, n), jnp.float32),
                pltpu.VMEM((n, n), jnp.float32),
            ],
        ),
        out_shape=jax.ShapeDtypeStruct((packed, NB), jnp.float32),
        compiler_params=pltpu.CompilerParams(vmem_limit_bytes=40 * 2**20),
        cost_estimate=pl.CostEstimate(
            flops=8 * capacity * rows * n * n, bytes_accessed=4 * capacity * rows * n, transcendentals=0
        ),
        name="local_gram",
    )(count, tiles, inverse_factor)


def sum_kernel(scenes, rows, g_ref, note_ref, out_ref, notes_ref, h0, h1, rx0, rx1, rx2, ss, rs):
    packed = g_ref.shape[0]
    half, part, chunk = packed // 2, packed // rows, packed // rows // scenes
    mates = rows // 2
    scene = lax.axis_index("scene")
    row = lax.axis_index("rows")
    core = lax.rem(row, 2)
    mate = lax.div(row, 2)
    pair = (scene, row + 1 - 2 * core)
    plane = [(scene, lax.rem(mate + d, mates) * 2 + core) for d in range(1, mates)]
    line = [(lax.rem(scene + d, scenes), row) for d in range(1, scenes)]

    barrier = pltpu.get_barrier_semaphore()
    peers = [pair] + plane + line
    for peer in peers:
        pl.semaphore_signal(barrier, inc=1, device_id=peer, device_id_type=pl.DeviceIdType.MESH)
    pl.semaphore_wait(barrier, len(peers))

    used = [0]

    def send(src, dst, peer):
        k = used[0]
        used[0] += 1
        copy = pltpu.make_async_remote_copy(
            src_ref=src, dst_ref=dst, send_sem=ss.at[k], recv_sem=rs.at[k],
            device_id=peer, device_id_type=pl.DeviceIdType.MESH,
        )
        copy.start()
        return copy

    def span(start, size):
        return pl.ds(pl.multiple_of(start, 8), size)

    copy = send(g_ref.at[span((1 - core) * half, half)], rx0, pair)
    copy.wait()
    h0[...] = g_ref[span(core * half, half), :] + rx0[...]

    copies = [send(h0.at[span(p[1] // 2 * part, part)], rx1.at[d], p) for d, p in enumerate(plane)]
    total = h0[span(mate * part, part), :]
    for d, copy in enumerate(copies):
        copy.wait()
        total += rx1[d]
    h1[...] = total

    copies = [send(h1.at[span(p[0] * chunk, chunk)], rx2.at[d], p) for d, p in enumerate(line)]
    notes = [send(note_ref, notes_ref.at[scene], p) for p in line]
    notes_ref[scene] = note_ref[...]
    total = h1[span(scene * chunk, chunk), :]
    for d, copy in enumerate(copies):
        copy.wait()
        total += rx2[d]

    mine = core * half + mate * part
    own = span(mine + scene * chunk, chunk)
    out_ref[own, :] = total
    for copy in [send(out_ref.at[own], out_ref.at[own], p) for p in line] + notes:
        copy.wait()
    own = span(mine, part)
    for copy in [send(out_ref.at[own], out_ref.at[own], p) for p in plane]:
        copy.wait()
    own = span(core * half, half)
    send(out_ref.at[own], out_ref.at[own], pair).wait()


def sum_all(gram, note, scenes, rows):
    packed = gram.shape[0]
    half, part, chunk = packed // 2, packed // rows, packed // rows // scenes
    copies = 2 + 2 * (rows // 2 - 1) + 3 * (scenes - 1)
    whole = pl.BlockSpec(memory_space=pltpu.VMEM)
    return pl.pallas_call(
        functools.partial(sum_kernel, scenes, rows),
        out_shape=[
            jax.ShapeDtypeStruct(gram.shape, gram.dtype),
            jax.ShapeDtypeStruct((scenes,) + note.shape, note.dtype),
        ],
        in_specs=[whole, whole],
        out_specs=[whole, whole],
        scratch_shapes=[
            pltpu.VMEM((half, NB), jnp.float32),
            pltpu.VMEM((part, NB), jnp.float32),
            pltpu.VMEM((half, NB), jnp.float32),
            pltpu.VMEM((rows // 2 - 1, part, NB), jnp.float32),
            pltpu.VMEM((scenes - 1, chunk, NB), jnp.float32),
            pltpu.SemaphoreType.DMA((copies,)),
            pltpu.SemaphoreType.DMA((copies,)),
        ],
        compiler_params=pltpu.CompilerParams(
            collective_id=0, has_side_effects=True, vmem_limit_bytes=24 * 2**20
        ),
        cost_estimate=pl.CostEstimate(flops=10 * packed * NB, bytes_accessed=16 * packed * NB, transcendentals=0),
        name="sum_all",
    )(gram, note)


def eliminate(block):
    lane = lax.broadcasted_iota(jnp.int32, (8, NB), 1)
    sub = lax.broadcasted_iota(jnp.int32, (8, 1), 0)
    groups = [block[8 * g : 8 * g + 8, :] for g in range(NB // 8)]
    for j in range(NB - 1):
        first, r = divmod(j, 8)
        row = groups[first][r : r + 1, :]
        inverse = 1.0 / row[:, j : j + 1]
        here = lane == j
        row = jnp.where(here[:1], 1.0, row)
        for g in range(first if r < 7 else first + 1, NB // 8):
            c = groups[g]
            coef = c[:, j : j + 1] * inverse
            if g == first:
                live = sub > r
                coef = jnp.where(live, coef, 0.0)
                base = jnp.where(here & live, 0.0, c)
            else:
                base = jnp.where(here, 0.0, c)
            groups[g] = base - coef * row
    return jnp.concatenate(groups, axis=0)


def hdot(a, b, dims=((1,), (0,))):
    return lax.dot_general(
        a, b, (dims, ((), ())), precision=lax.Precision.HIGHEST, preferred_element_type=jnp.float32
    )


def factor_kernel(rows_all, g_ref, r_ref, u_ref, mh_ref, ml_ref, work):
    n = r_ref.shape[0]
    for b, (bi, bj) in enumerate(lower_blocks(n)):
        rows = slice(bi * NB, (bi + 1) * NB)
        cols = slice(bj * NB, (bj + 1) * NB)
        block = g_ref[b * NB : (b + 1) * NB, :] / rows_all
        work[rows, cols] = block
        if bi != bj:
            work[cols, rows] = block.T
    work[:, n:] = (
        lax.broadcasted_iota(jnp.int32, (n, n), 0) == lax.broadcasted_iota(jnp.int32, (n, n), 1)
    ).astype(jnp.float32)

    def step(k, carry):
        at = pl.multiple_of(k * NB, NB)
        here = pl.ds(at, NB)
        done = eliminate(work[here, here])
        i = lax.broadcasted_iota(jnp.int32, (NB, NB), 0)
        j = lax.broadcasted_iota(jnp.int32, (NB, NB), 1)
        scale = lax.rsqrt(jnp.sum(jnp.where(i == j, done, 0.0), axis=1, keepdims=True))
        inverse = jnp.where(i > j, done, jnp.where(i == j, 1.0, 0.0)) * scale
        panel = hdot(inverse, work[here, :])
        work[here, :] = panel
        work[here, here] = jnp.where(i <= j, done, 0.0) * scale
        column = lax.broadcasted_iota(jnp.int32, (NB, n), 1)
        coef = jnp.where(column >= at + NB, panel[:, :n], 0.0)

        @pl.when(k < n // NB - 1)
        def _():
            work[...] -= hdot(coef, panel, ((0,), (0,)))

        return carry

    lax.fori_loop(0, n // NB, step, 0)
    i = lax.broadcasted_iota(jnp.int32, (n, n), 0)
    j = lax.broadcasted_iota(jnp.int32, (n, n), 1)
    u_ref[...] = jnp.where(i <= j, work[:, :n], 0.0)
    m = hdot(r_ref[...], work[:, n:], ((1,), (1,)))
    h, l = split(m)
    mh_ref[...] = h
    ml_ref[...] = l


def factorise(gram, inverse_factor, rows_all):
    n = inverse_factor.shape[0]
    return pl.pallas_call(
        functools.partial(factor_kernel, rows_all),
        out_shape=[
            jax.ShapeDtypeStruct((n, n), jnp.float32),
            jax.ShapeDtypeStruct((n, n), jnp.bfloat16),
            jax.ShapeDtypeStruct((n, n), jnp.bfloat16),
        ],
        in_specs=[pl.BlockSpec(memory_space=pltpu.VMEM)] * 2,
        out_specs=[pl.BlockSpec(memory_space=pltpu.VMEM)] * 3,
        scratch_shapes=[pltpu.VMEM((n, 2 * n), jnp.float32)],
        compiler_params=pltpu.CompilerParams(vmem_limit_bytes=40 * 2**20),
        cost_estimate=pl.CostEstimate(flops=40 * n**3, bytes_accessed=16 * n * n, transcendentals=0),
        name="factorise",
    )(gram, inverse_factor)


def last_kernel(index_ref, first_ref, rest_ref, mh_ref, ml_ref, o_ref):
    x = jnp.concatenate([first_ref[0], rest_ref[0]], axis=0)
    a, b = upper_product(x, mh_ref[...], ml_ref[...])
    o_ref[0, :, :HALF] = a
    o_ref[0, :, HALF:] = b


def last_product(index, first, rest, mh, ml):
    n = first.shape[2]
    rows = first.shape[1] + rest.shape[1]
    whole = pl.BlockSpec((n, n), lambda i, idx: (0, 0))

    def tiles(x):
        return pl.BlockSpec((1,) + x.shape[1:], lambda i, idx: (idx[i], 0, 0))

    return pl.pallas_call(
        last_kernel,
        grid_spec=pltpu.PrefetchScalarGridSpec(
            num_scalar_prefetch=1,
            grid=(OWN_TILES,),
            in_specs=[tiles(first), tiles(rest), whole, whole],
            out_specs=pl.BlockSpec((1, rows, n), lambda i, idx: (i, 0, 0)),
        ),
        out_shape=jax.ShapeDtypeStruct((OWN_TILES, rows, n), jnp.float32),
        compiler_params=pltpu.CompilerParams(vmem_limit_bytes=32 * 2**20),
        name="last_product",
    )(index, first, rest, mh, ml)


def seats(owner, count, scenes):
    capacity = owner.shape[0]
    position = jnp.arange(capacity, dtype=jnp.int32)
    is_live = position < count
    earlier = (owner[:, None] == owner[None, :]) & is_live[None, :] & (position[None, :] < position[:, None])
    rank = earlier.astype(jnp.int32).sum(1)
    return is_live, rank


def shards(observations, inverse_factor, tile_count, tile_owner, tile_slot):
    scenes = lax.axis_size("scene")
    devices = scenes * lax.axis_size("rows")
    capacity = tile_owner.shape[0]
    pair_most = capacity // scenes
    tile_rows, n = observations.shape[1:]
    position = jnp.arange(capacity, dtype=jnp.int32)

    is_live, rank = seats(tile_owner, tile_count[0], scenes)
    target = jnp.where(is_live, tile_owner * pair_most + rank, -1)
    selector = (target[None, :] == position[:, None]).astype(jnp.int32)
    chosen = (selector * position[None, :]).sum(1)

    def exchange(outgoing):
        rows = outgoing.shape[1]
        return lax.all_to_all(
            outgoing.reshape(scenes, pair_most, rows, n), "scene", split_axis=0, concat_axis=0, tiled=True
        ).reshape(capacity, rows, n)

    first, count = lax.optimization_barrier((gather_rows(chosen, observations, 0, FIRST), tile_count))
    first = exchange(first)
    rest = gather_rows(chosen, observations, FIRST, tile_rows - FIRST)

    me = lax.axis_index("scene")
    note = jnp.where(is_live, (tile_owner * pair_most + rank) * OWN_TILES + tile_slot, -1)
    note = jnp.zeros((8, 128), jnp.int32).at[0, :capacity].set(note)
    chunk = -(-len(lower_blocks(n)) * NB // devices // 8) * 8
    gram = local_gram(count, observations, inverse_factor, chunk * devices)
    gram, notes = sum_all(gram, note, scenes, lax.axis_size("rows"))
    rest, gram = lax.optimization_barrier((rest, gram))
    rest = exchange(rest)
    notes = notes[:, 0, :capacity]
    seat = notes // OWN_TILES
    mine = (notes >= 0) & (seat // pair_most == me)
    place = jnp.arange(scenes, dtype=jnp.int32)[:, None] * pair_most + seat % pair_most
    match = mine[None] & ((notes % OWN_TILES)[None] == jnp.arange(OWN_TILES, dtype=jnp.int32)[:, None, None])
    order = jnp.where(match, place[None], 0).sum((1, 2))

    factor, mh, ml = factorise(gram, inverse_factor, devices * OWN_TILES * tile_rows)
    return last_product(order, first, rest, mh, ml), factor


def solution(mesh):
    in_specs = (
        P(("scene", "rows"), None, None),
        P(),
        P(("scene", "rows")),
        P(("scene", "rows")),
        P(("scene", "rows")),
    )
    out_specs = (P(("scene", "rows"), None, None), P())
    return jax.shard_map(shards, mesh=mesh, in_specs=in_specs, out_specs=out_specs, check_vma=False)
```

```python
import functools

import jax
import jax.numpy as jnp
from jax import lax
from jax.experimental import pallas as pl
from jax.experimental.pallas import tpu as pltpu
from jax.sharding import PartitionSpec as P

OWN_TILES = 8
NB = 128
HALF = 256
FIRST = 64
LAST = 64
PER_STEP = 4


def split(x):
    hi = x.astype(jnp.bfloat16)
    return hi, (x - hi.astype(jnp.float32)).astype(jnp.bfloat16)


def mm(a, b):
    return jnp.dot(a, b, preferred_element_type=jnp.float32)


def upper_product(x, uh, ul):
    xh, xl = split(x)
    left = slice(0, HALF)
    right = slice(HALF, None)
    a = mm(xh[:, left], uh[left, left]) + (mm(xh[:, left], ul[left, left]) + mm(xl[:, left], uh[left, left]))
    b = mm(xh, uh[:, right]) + (mm(xh, ul[:, right]) + mm(xl, uh[:, right]))
    return a, b


def copy_kernel(starts, index_ref, x_ref, *refs):
    outs, sems = refs[:-1], refs[-1]
    copies = []
    for p, (start, o_ref) in enumerate(zip(starts, outs)):
        for i in range(o_ref.shape[0]):
            source = x_ref.at[index_ref[i], pl.ds(start, o_ref.shape[1]), :]
            copies.append(pltpu.make_async_copy(source, o_ref.at[i], sems.at[p, i]))
    for copy in copies:
        copy.start()
    for copy in copies:
        copy.wait()


def gather_rows(index, tiles, spans):
    count = index.shape[0]
    anywhere = pl.BlockSpec(memory_space=pl.ANY)
    return pl.pallas_call(
        functools.partial(copy_kernel, [start for start, _ in spans]),
        in_specs=[pl.BlockSpec(memory_space=pltpu.SMEM), anywhere],
        out_specs=[anywhere] * len(spans),
        out_shape=[jax.ShapeDtypeStruct((count, rows, tiles.shape[2]), tiles.dtype) for _, rows in spans],
        scratch_shapes=[pltpu.SemaphoreType.DMA((len(spans), count))],
        name="gather_rows",
    )(index, tiles)


def lower_blocks(n):
    return [(i, j) for i in range(n // NB) for j in range(i + 1)]


def gram_kernel(count_ref, x_ref, r_ref, g_ref, rh, rl, low, cross):
    i = pl.program_id(0)

    @pl.when(i == 0)
    def _():
        h, l = split(r_ref[...])
        rh[...] = h
        rl[...] = l
        low[...] = jnp.zeros_like(low)
        cross[...] = jnp.zeros_like(cross)

    @pl.when(i < count_ref[0])
    def _():
        a, b = upper_product(x_ref[0], rh[...], rl[...])
        ah, al = split(a)
        bh, bl = split(b)
        at = ah.T
        bt = bh.T
        low[:HALF, :HALF] += mm(at, ah)
        low[HALF:, :HALF] += mm(bt, ah)
        low[HALF:, HALF:] += mm(bt, bh)
        cross[:HALF, :HALF] += mm(at, al)
        cross[:HALF, HALF:] += mm(at, bl)
        cross[HALF:, :HALF] += mm(bt, al)
        cross[HALF:, HALF:] += mm(bt, bl)

    @pl.when(i == pl.num_programs(0) - 1)
    def _():
        blocks = lower_blocks(low.shape[0])
        for k, (bi, bj) in enumerate(blocks):
            rows = slice(bi * NB, (bi + 1) * NB)
            cols = slice(bj * NB, (bj + 1) * NB)
            g_ref[k * NB : (k + 1) * NB, :] = low[rows, cols] + (cross[rows, cols] + cross[cols, rows].T)
        used = len(blocks) * NB
        if used < g_ref.shape[0]:
            g_ref[used:, :] = jnp.zeros((g_ref.shape[0] - used, NB), jnp.float32)


def local_gram(count, tiles, inverse_factor, packed):
    capacity, rows, n = tiles.shape
    return pl.pallas_call(
        gram_kernel,
        grid_spec=pltpu.PrefetchScalarGridSpec(
            num_scalar_prefetch=1,
            grid=(capacity,),
            in_specs=[
                pl.BlockSpec(
                    (1, rows, n), lambda i, c: (jnp.minimum(i, jnp.maximum(c[0] - 1, 0)), 0, 0)
                ),
                pl.BlockSpec((n, n), lambda i, c: (0, 0)),
            ],
            out_specs=pl.BlockSpec((packed, NB), lambda i, c: (0, 0)),
            scratch_shapes=[
                pltpu.VMEM((n, n), jnp.bfloat16),
                pltpu.VMEM((n, n), jnp.bfloat16),
                pltpu.VMEM((n, n), jnp.float32),
                pltpu.VMEM((n, n), jnp.float32),
            ],
        ),
        out_shape=jax.ShapeDtypeStruct((packed, NB), jnp.float32),
        compiler_params=pltpu.CompilerParams(vmem_limit_bytes=40 * 2**20),
        cost_estimate=pl.CostEstimate(
            flops=8 * capacity * rows * n * n, bytes_accessed=4 * capacity * rows * n, transcendentals=0
        ),
        name="local_gram",
    )(count, tiles, inverse_factor)


def place():
    row = lax.axis_index("rows")
    return lax.axis_index("scene"), row, lax.rem(row, 2), lax.div(row, 2)


def greet(peers):
    barrier = pltpu.get_barrier_semaphore()
    for peer in peers:
        pl.semaphore_signal(barrier, inc=1, device_id=peer, device_id_type=pl.DeviceIdType.MESH)
    pl.semaphore_wait(barrier, len(peers))


def sender(ss, rs):
    used = [0]

    def send(src, dst, peer):
        k = used[0]
        used[0] += 1
        copy = pltpu.make_async_remote_copy(
            src_ref=src, dst_ref=dst, send_sem=ss.at[k], recv_sem=rs.at[k],
            device_id=peer, device_id_type=pl.DeviceIdType.MESH,
        )
        copy.start()
        return copy

    return send


def span(start, size):
    return pl.ds(pl.multiple_of(start, 8), size)


def sum_kernel(scenes, rows, g_ref, note_ref, out_ref, notes_ref, h0, h1, rx0, rx1, rx2, ss, rs):
    packed = g_ref.shape[0]
    half, part, chunk = packed // 2, packed // rows, packed // rows // scenes
    mates = rows // 2
    scene, row, core, mate = place()
    pair = (scene, row + 1 - 2 * core)
    plane = [(scene, lax.rem(mate + d, mates) * 2 + core) for d in range(1, mates)]
    line = [(lax.rem(scene + d, scenes), row) for d in range(1, scenes)]
    greet([pair] + plane + line)
    send = sender(ss, rs)

    copy = send(g_ref.at[span((1 - core) * half, half)], rx0, pair)
    copy.wait()
    h0[...] = g_ref[span(core * half, half), :] + rx0[...]

    copies = [send(h0.at[span(lax.div(p[1], 2) * part, part)], rx1.at[d], p) for d, p in enumerate(plane)]
    total = h0[span(mate * part, part), :]
    for d, copy in enumerate(copies):
        copy.wait()
        total += rx1[d]
    h1[...] = total

    copies = [send(h1.at[span(p[0] * chunk, chunk)], rx2.at[d], p) for d, p in enumerate(line)]
    notes = [send(note_ref, notes_ref.at[scene], p) for p in line]
    notes_ref[scene] = note_ref[...]
    total = h1[span(scene * chunk, chunk), :]
    for d, copy in enumerate(copies):
        copy.wait()
        total += rx2[d]

    own = span(scene * chunk, chunk)
    out_ref[own, :] = total
    for copy in [send(out_ref.at[own], out_ref.at[own], p) for p in line] + notes:
        copy.wait()


def sum_part(gram, note, scenes, rows):
    packed = gram.shape[0]
    half, part, chunk = packed // 2, packed // rows, packed // rows // scenes
    copies = rows // 2 + 3 * (scenes - 1)
    whole = pl.BlockSpec(memory_space=pltpu.VMEM)
    return pl.pallas_call(
        functools.partial(sum_kernel, scenes, rows),
        out_shape=[
            jax.ShapeDtypeStruct((part, NB), gram.dtype),
            jax.ShapeDtypeStruct((scenes,) + note.shape, note.dtype),
        ],
        in_specs=[whole, whole],
        out_specs=[whole, whole],
        scratch_shapes=[
            pltpu.VMEM((half, NB), jnp.float32),
            pltpu.VMEM((part, NB), jnp.float32),
            pltpu.VMEM((half, NB), jnp.float32),
            pltpu.VMEM((rows // 2 - 1, part, NB), jnp.float32),
            pltpu.VMEM((scenes - 1, chunk, NB), jnp.float32),
            pltpu.SemaphoreType.DMA((copies,)),
            pltpu.SemaphoreType.DMA((copies,)),
        ],
        compiler_params=pltpu.CompilerParams(
            collective_id=0, has_side_effects=True, vmem_limit_bytes=24 * 2**20
        ),
        cost_estimate=pl.CostEstimate(flops=10 * packed * NB, bytes_accessed=16 * packed * NB, transcendentals=0),
        name="sum_part",
    )(gram, note)


def spread_kernel(rows, h_ref, out_ref, ss, rs):
    packed = out_ref.shape[0]
    half, part = packed // 2, packed // rows
    mates = rows // 2
    scene, row, core, mate = place()
    pair = (scene, row + 1 - 2 * core)
    plane = [(scene, lax.rem(mate + d, mates) * 2 + core) for d in range(1, mates)]
    greet([pair] + plane)
    send = sender(ss, rs)
    own = span(core * half + mate * part, part)
    copies = [send(h_ref, out_ref.at[own], p) for p in plane]
    out_ref[own, :] = h_ref[...]
    for copy in copies:
        copy.wait()
    own = span(core * half, half)
    send(out_ref.at[own], out_ref.at[own], pair).wait()


def spread(part_sum, rows):
    whole = pl.BlockSpec(memory_space=pltpu.VMEM)
    packed = part_sum.shape[0] * rows
    return pl.pallas_call(
        functools.partial(spread_kernel, rows),
        out_shape=jax.ShapeDtypeStruct((packed, NB), part_sum.dtype),
        in_specs=[whole],
        out_specs=whole,
        scratch_shapes=[pltpu.SemaphoreType.DMA((rows // 2,)), pltpu.SemaphoreType.DMA((rows // 2,))],
        compiler_params=pltpu.CompilerParams(
            collective_id=1, has_side_effects=True, vmem_limit_bytes=24 * 2**20
        ),
        cost_estimate=pl.CostEstimate(flops=packed * NB, bytes_accessed=8 * packed * NB, transcendentals=0),
        name="spread",
    )(part_sum)


def eliminate(block):
    lane = lax.broadcasted_iota(jnp.int32, (8, NB), 1)
    sub = lax.broadcasted_iota(jnp.int32, (8, 1), 0)
    groups = [block[8 * g : 8 * g + 8, :] for g in range(NB // 8)]
    for j in range(NB - 1):
        first, r = divmod(j, 8)
        row = groups[first][r : r + 1, :]
        inverse = 1.0 / row[:, j : j + 1]
        here = lane == j
        row = jnp.where(here[:1], 1.0, row)
        for g in range(first if r < 7 else first + 1, NB // 8):
            c = groups[g]
            coef = c[:, j : j + 1] * inverse
            if g == first:
                live = sub > r
                coef = jnp.where(live, coef, 0.0)
                base = jnp.where(here & live, 0.0, c)
            else:
                base = jnp.where(here, 0.0, c)
            groups[g] = base - coef * row
    return jnp.concatenate(groups, axis=0)


def hdot(a, b, dims=((1,), (0,))):
    return lax.dot_general(
        a, b, (dims, ((), ())), precision=lax.Precision.HIGHEST, preferred_element_type=jnp.float32
    )


def factor_kernel(rows_all, g_ref, r_ref, u_ref, mh_ref, ml_ref, work):
    n = r_ref.shape[0]
    for b, (bi, bj) in enumerate(lower_blocks(n)):
        rows = slice(bi * NB, (bi + 1) * NB)
        cols = slice(bj * NB, (bj + 1) * NB)
        block = g_ref[b * NB : (b + 1) * NB, :] / rows_all
        work[rows, cols] = block
        if bi != bj:
            work[cols, rows] = block.T
    work[:, n:] = (
        lax.broadcasted_iota(jnp.int32, (n, n), 0) == lax.broadcasted_iota(jnp.int32, (n, n), 1)
    ).astype(jnp.float32)

    def step(k, carry):
        at = pl.multiple_of(k * NB, NB)
        here = pl.ds(at, NB)
        done = eliminate(work[here, here])
        i = lax.broadcasted_iota(jnp.int32, (NB, NB), 0)
        j = lax.broadcasted_iota(jnp.int32, (NB, NB), 1)
        scale = lax.rsqrt(jnp.sum(jnp.where(i == j, done, 0.0), axis=1, keepdims=True))
        inverse = jnp.where(i > j, done, jnp.where(i == j, 1.0, 0.0)) * scale
        panel = hdot(inverse, work[here, :])
        work[here, :] = panel
        work[here, here] = jnp.where(i <= j, done, 0.0) * scale
        column = lax.broadcasted_iota(jnp.int32, (NB, n), 1)
        coef = jnp.where(column >= at + NB, panel[:, :n], 0.0)

        @pl.when(k < n // NB - 1)
        def _():
            work[...] -= hdot(coef, panel, ((0,), (0,)))

        return carry

    lax.fori_loop(0, n // NB, step, 0)
    i = lax.broadcasted_iota(jnp.int32, (n, n), 0)
    j = lax.broadcasted_iota(jnp.int32, (n, n), 1)
    u_ref[...] = jnp.where(i <= j, work[:, :n], 0.0)
    m = hdot(r_ref[...], work[:, n:], ((1,), (1,)))
    h, l = split(m)
    mh_ref[...] = h
    ml_ref[...] = l


def factorise(gram, inverse_factor, rows_all):
    n = inverse_factor.shape[0]
    return pl.pallas_call(
        functools.partial(factor_kernel, rows_all),
        out_shape=[
            jax.ShapeDtypeStruct((n, n), jnp.float32),
            jax.ShapeDtypeStruct((n, n), jnp.bfloat16),
            jax.ShapeDtypeStruct((n, n), jnp.bfloat16),
        ],
        in_specs=[pl.BlockSpec(memory_space=pltpu.VMEM)] * 2,
        out_specs=[pl.BlockSpec(memory_space=pltpu.VMEM)] * 3,
        scratch_shapes=[pltpu.VMEM((n, 2 * n), jnp.float32)],
        compiler_params=pltpu.CompilerParams(vmem_limit_bytes=40 * 2**20),
        cost_estimate=pl.CostEstimate(flops=40 * n**3, bytes_accessed=16 * n * n, transcendentals=0),
        name="factorise",
    )(gram, inverse_factor)


def last_kernel(pieces, index_ref, *refs):
    mh_ref, ml_ref = refs[PER_STEP * pieces : PER_STEP * pieces + 2]
    o_ref = refs[-1]
    x = jnp.concatenate([r[0] for r in refs[: PER_STEP * pieces]], axis=0)
    a, b = upper_product(x, mh_ref[...], ml_ref[...])
    shape = (PER_STEP, o_ref.shape[1], HALF)
    o_ref[:, :, :HALF] = a.reshape(shape)
    o_ref[:, :, HALF:] = b.reshape(shape)


def last_product(index, pieces, mh, ml, tile_rows, block, before=None):
    n = mh.shape[0]
    rows = sum(x.shape[1] for x in pieces)
    whole = pl.BlockSpec((n, n), lambda i, idx: (0, 0))

    def tile(x, t):
        return pl.BlockSpec((1,) + x.shape[1:], lambda i, idx: (idx[i * PER_STEP + t], 0, 0))

    operands = [x for _ in range(PER_STEP) for x in pieces] + [mh, ml]
    specs = [tile(x, t) for t in range(PER_STEP) for x in pieces] + [whole, whole]
    aliases = {}
    if before is not None:
        aliases = {1 + len(operands): 0}
        operands.append(before)
        specs.append(pl.BlockSpec(memory_space=pl.ANY))
    return pl.pallas_call(
        functools.partial(last_kernel, len(pieces)),
        grid_spec=pltpu.PrefetchScalarGridSpec(
            num_scalar_prefetch=1,
            grid=(OWN_TILES // PER_STEP,),
            in_specs=specs,
            out_specs=pl.BlockSpec((PER_STEP, rows, n), lambda i, idx: (i, block, 0)),
        ),
        out_shape=jax.ShapeDtypeStruct((OWN_TILES, tile_rows, n), jnp.float32),
        input_output_aliases=aliases,
        compiler_params=pltpu.CompilerParams(vmem_limit_bytes=40 * 2**20),
        cost_estimate=pl.CostEstimate(
            flops=6 * OWN_TILES * rows * n * n, bytes_accessed=8 * OWN_TILES * rows * n, transcendentals=0
        ),
        name="last_product",
    )(index, *operands)


def seats(owner, count, scenes):
    capacity = owner.shape[0]
    position = jnp.arange(capacity, dtype=jnp.int32)
    is_live = position < count
    earlier = (owner[:, None] == owner[None, :]) & is_live[None, :] & (position[None, :] < position[:, None])
    rank = earlier.astype(jnp.int32).sum(1)
    return is_live, rank


def shards(observations, inverse_factor, tile_count, tile_owner, tile_slot):
    scenes = lax.axis_size("scene")
    devices = scenes * lax.axis_size("rows")
    capacity = tile_owner.shape[0]
    pair_most = capacity // scenes
    tile_rows, n = observations.shape[1:]
    position = jnp.arange(capacity, dtype=jnp.int32)

    is_live, rank = seats(tile_owner, tile_count[0], scenes)
    target = jnp.where(is_live, tile_owner * pair_most + rank, -1)
    selector = (target[None, :] == position[:, None]).astype(jnp.int32)
    chosen = (selector * position[None, :]).sum(1)

    def exchange(outgoing):
        rows = outgoing.shape[1]
        return lax.all_to_all(
            outgoing.reshape(scenes, pair_most, rows, n), "scene", split_axis=0, concat_axis=0, tiled=True
        ).reshape(capacity, rows, n)

    first, count = lax.optimization_barrier((gather_rows(chosen, observations, [(0, FIRST)])[0], tile_count))
    first = exchange(first)
    middle, rest = gather_rows(
        chosen, observations, [(FIRST, tile_rows - FIRST - LAST), (tile_rows - LAST, LAST)]
    )

    me = lax.axis_index("scene")
    note = jnp.where(is_live, (tile_owner * pair_most + rank) * OWN_TILES + tile_slot, -1)
    note = jnp.zeros((8, 128), jnp.int32).at[0, :capacity].set(note)
    chunk = -(-len(lower_blocks(n)) * NB // devices // 8) * 8
    gram = local_gram(count, observations, inverse_factor, chunk * devices)
    rows = lax.axis_size("rows")
    part_sum, notes = sum_part(gram, note, scenes, rows)
    middle, rest, part_sum = lax.optimization_barrier((middle, rest, part_sum))
    middle = exchange(middle)
    rest = exchange(rest)
    gram = spread(part_sum, rows)
    notes = notes[:, 0, :capacity]
    seat = notes // OWN_TILES
    mine = (notes >= 0) & (seat // pair_most == me)
    place = jnp.arange(scenes, dtype=jnp.int32)[:, None] * pair_most + seat % pair_most
    match = mine[None] & ((notes % OWN_TILES)[None] == jnp.arange(OWN_TILES, dtype=jnp.int32)[:, None, None])
    order = jnp.where(match, place[None], 0).sum((1, 2))

    factor, mh, ml = factorise(gram, inverse_factor, devices * OWN_TILES * tile_rows)
    most = last_product(order, [first, middle], mh, ml, tile_rows, 0)
    return last_product(order, [rest], mh, ml, tile_rows, tile_rows // LAST - 1, most), factor


def solution(mesh):
    in_specs = (
        P(("scene", "rows"), None, None),
        P(),
        P(("scene", "rows")),
        P(("scene", "rows")),
        P(("scene", "rows")),
    )
    out_specs = (P(("scene", "rows"), None, None), P())
    return jax.shard_map(shards, mesh=mesh, in_specs=in_specs, out_specs=out_specs, check_vma=False)
```

```python
import functools

import jax
import jax.numpy as jnp
from jax import lax
from jax.experimental import pallas as pl
from jax.experimental.pallas import tpu as pltpu
from jax.sharding import PartitionSpec as P

OWN_TILES = 8
NB = 128
HALF = 256
FIRST = 64
PER_STEP = 4


def split(x):
    hi = x.astype(jnp.bfloat16)
    return hi, (x - hi.astype(jnp.float32)).astype(jnp.bfloat16)


def mm(a, b):
    return jnp.dot(a, b, preferred_element_type=jnp.float32)


def upper_product(x, uh, ul):
    xh, xl = split(x)
    left = slice(0, HALF)
    right = slice(HALF, None)
    a = mm(xh[:, left], uh[left, left]) + (mm(xh[:, left], ul[left, left]) + mm(xl[:, left], uh[left, left]))
    b = mm(xh, uh[:, right]) + (mm(xh, ul[:, right]) + mm(xl, uh[:, right]))
    return a, b


def copy_kernel(start, index_ref, x_ref, o_ref, held, in_sems, out_sems):
    count, rows = o_ref.shape[:2]

    def read(i):
        return pltpu.make_async_copy(x_ref.at[index_ref[i], pl.ds(start, rows), :], held.at[i], in_sems.at[i])

    def write(i):
        return pltpu.make_async_copy(held.at[i], o_ref.at[i], out_sems.at[i])

    for i in range(count):
        read(i).start()
    for i in range(count):
        read(i).wait()
        write(i).start()
    for i in range(count):
        write(i).wait()


def gather_rows(index, tiles, start, rows):
    shape = (index.shape[0], rows, tiles.shape[2])
    anywhere = pl.BlockSpec(memory_space=pl.ANY)
    return pl.pallas_call(
        functools.partial(copy_kernel, start),
        in_specs=[pl.BlockSpec(memory_space=pltpu.SMEM), anywhere],
        out_specs=anywhere,
        out_shape=jax.ShapeDtypeStruct(shape, tiles.dtype),
        scratch_shapes=[
            pltpu.VMEM(shape, tiles.dtype),
            pltpu.SemaphoreType.DMA((shape[0],)),
            pltpu.SemaphoreType.DMA((shape[0],)),
        ],
        compiler_params=pltpu.CompilerParams(vmem_limit_bytes=24 * 2**20),
        name="gather_rows",
    )(index, tiles)


def lower_blocks(n):
    return [(i, j) for i in range(n // NB) for j in range(i + 1)]


def gram_kernel(count_ref, x_ref, r_ref, g_ref, rh, rl, low, cross):
    i = pl.program_id(0)

    @pl.when(i == 0)
    def _():
        h, l = split(r_ref[...])
        rh[...] = h
        rl[...] = l
        low[...] = jnp.zeros_like(low)
        cross[...] = jnp.zeros_like(cross)

    @pl.when(i < count_ref[0])
    def _():
        a, b = upper_product(x_ref[0], rh[...], rl[...])
        ah, al = split(a)
        bh, bl = split(b)
        at = ah.T
        bt = bh.T
        low[:HALF, :HALF] += mm(at, ah)
        low[HALF:, :HALF] += mm(bt, ah)
        low[HALF:, HALF:] += mm(bt, bh)
        cross[:HALF, :HALF] += mm(at, al)
        cross[:HALF, HALF:] += mm(at, bl)
        cross[HALF:, :HALF] += mm(bt, al)
        cross[HALF:, HALF:] += mm(bt, bl)

    @pl.when(i == pl.num_programs(0) - 1)
    def _():
        blocks = lower_blocks(low.shape[0])
        for k, (bi, bj) in enumerate(blocks):
            rows = slice(bi * NB, (bi + 1) * NB)
            cols = slice(bj * NB, (bj + 1) * NB)
            g_ref[k * NB : (k + 1) * NB, :] = low[rows, cols] + (cross[rows, cols] + cross[cols, rows].T)
        used = len(blocks) * NB
        if used < g_ref.shape[0]:
            g_ref[used:, :] = jnp.zeros((g_ref.shape[0] - used, NB), jnp.float32)


def local_gram(count, tiles, inverse_factor, packed):
    capacity, rows, n = tiles.shape
    return pl.pallas_call(
        gram_kernel,
        grid_spec=pltpu.PrefetchScalarGridSpec(
            num_scalar_prefetch=1,
            grid=(capacity,),
            in_specs=[
                pl.BlockSpec(
                    (1, rows, n), lambda i, c: (jnp.minimum(i, jnp.maximum(c[0] - 1, 0)), 0, 0)
                ),
                pl.BlockSpec((n, n), lambda i, c: (0, 0)),
            ],
            out_specs=pl.BlockSpec((packed, NB), lambda i, c: (0, 0)),
            scratch_shapes=[
                pltpu.VMEM((n, n), jnp.bfloat16),
                pltpu.VMEM((n, n), jnp.bfloat16),
                pltpu.VMEM((n, n), jnp.float32),
                pltpu.VMEM((n, n), jnp.float32),
            ],
        ),
        out_shape=jax.ShapeDtypeStruct((packed, NB), jnp.float32),
        compiler_params=pltpu.CompilerParams(vmem_limit_bytes=40 * 2**20),
        cost_estimate=pl.CostEstimate(
            flops=8 * capacity * rows * n * n, bytes_accessed=4 * capacity * rows * n, transcendentals=0
        ),
        name="local_gram",
    )(count, tiles, inverse_factor)


def place():
    row = lax.axis_index("rows")
    return lax.axis_index("scene"), row, lax.rem(row, 2), lax.div(row, 2)


def greet(peers):
    barrier = pltpu.get_barrier_semaphore()
    for peer in peers:
        pl.semaphore_signal(barrier, inc=1, device_id=peer, device_id_type=pl.DeviceIdType.MESH)
    pl.semaphore_wait(barrier, len(peers))


def sender(ss, rs):
    used = [0]

    def send(src, dst, peer):
        k = used[0]
        used[0] += 1
        copy = pltpu.make_async_remote_copy(
            src_ref=src, dst_ref=dst, send_sem=ss.at[k], recv_sem=rs.at[k],
            device_id=peer, device_id_type=pl.DeviceIdType.MESH,
        )
        copy.start()
        return copy

    return send


def span(start, size):
    return pl.ds(pl.multiple_of(start, 8), size)


def sum_kernel(scenes, rows, g_ref, note_ref, out_ref, notes_ref, h0, h1, rx0, rx1, rx2, ss, rs):
    packed = g_ref.shape[0]
    half, part, chunk = packed // 2, packed // rows, packed // rows // scenes
    mates = rows // 2
    scene, row, core, mate = place()
    pair = (scene, row + 1 - 2 * core)
    plane = [(scene, lax.rem(mate + d, mates) * 2 + core) for d in range(1, mates)]
    line = [(lax.rem(scene + d, scenes), row) for d in range(1, scenes)]
    greet([pair] + plane + line)
    send = sender(ss, rs)

    copy = send(g_ref.at[span((1 - core) * half, half)], rx0, pair)
    copy.wait()
    h0[...] = g_ref[span(core * half, half), :] + rx0[...]

    copies = [send(h0.at[span(lax.div(p[1], 2) * part, part)], rx1.at[d], p) for d, p in enumerate(plane)]
    total = h0[span(mate * part, part), :]
    for d, copy in enumerate(copies):
        copy.wait()
        total += rx1[d]
    h1[...] = total

    copies = [send(h1.at[span(p[0] * chunk, chunk)], rx2.at[d], p) for d, p in enumerate(line)]
    notes = [send(note_ref, notes_ref.at[scene], p) for p in line]
    notes_ref[scene] = note_ref[...]
    total = h1[span(scene * chunk, chunk), :]
    for d, copy in enumerate(copies):
        copy.wait()
        total += rx2[d]

    own = span(scene * chunk, chunk)
    out_ref[own, :] = total
    for copy in [send(out_ref.at[own], out_ref.at[own], p) for p in line] + notes:
        copy.wait()


def sum_part(gram, note, scenes, rows):
    packed = gram.shape[0]
    half, part, chunk = packed // 2, packed // rows, packed // rows // scenes
    copies = rows // 2 + 3 * (scenes - 1)
    whole = pl.BlockSpec(memory_space=pltpu.VMEM)
    return pl.pallas_call(
        functools.partial(sum_kernel, scenes, rows),
        out_shape=[
            jax.ShapeDtypeStruct((part, NB), gram.dtype),
            jax.ShapeDtypeStruct((scenes,) + note.shape, note.dtype),
        ],
        in_specs=[whole, whole],
        out_specs=[whole, whole],
        scratch_shapes=[
            pltpu.VMEM((half, NB), jnp.float32),
            pltpu.VMEM((part, NB), jnp.float32),
            pltpu.VMEM((half, NB), jnp.float32),
            pltpu.VMEM((rows // 2 - 1, part, NB), jnp.float32),
            pltpu.VMEM((scenes - 1, chunk, NB), jnp.float32),
            pltpu.SemaphoreType.DMA((copies,)),
            pltpu.SemaphoreType.DMA((copies,)),
        ],
        compiler_params=pltpu.CompilerParams(
            collective_id=0, has_side_effects=True, vmem_limit_bytes=24 * 2**20
        ),
        cost_estimate=pl.CostEstimate(flops=10 * packed * NB, bytes_accessed=16 * packed * NB, transcendentals=0),
        name="sum_part",
    )(gram, note)


def spread_kernel(rows, h_ref, out_ref, ss, rs):
    packed = out_ref.shape[0]
    half, part = packed // 2, packed // rows
    mates = rows // 2
    scene, row, core, mate = place()
    pair = (scene, row + 1 - 2 * core)
    plane = [(scene, lax.rem(mate + d, mates) * 2 + core) for d in range(1, mates)]
    greet([pair] + plane)
    send = sender(ss, rs)
    own = span(core * half + mate * part, part)
    copies = [send(h_ref, out_ref.at[own], p) for p in plane]
    out_ref[own, :] = h_ref[...]
    for copy in copies:
        copy.wait()
    own = span(core * half, half)
    send(out_ref.at[own], out_ref.at[own], pair).wait()


def spread(part_sum, rows):
    whole = pl.BlockSpec(memory_space=pltpu.VMEM)
    packed = part_sum.shape[0] * rows
    return pl.pallas_call(
        functools.partial(spread_kernel, rows),
        out_shape=jax.ShapeDtypeStruct((packed, NB), part_sum.dtype),
        in_specs=[whole],
        out_specs=whole,
        scratch_shapes=[pltpu.SemaphoreType.DMA((rows // 2,)), pltpu.SemaphoreType.DMA((rows // 2,))],
        compiler_params=pltpu.CompilerParams(
            collective_id=1, has_side_effects=True, vmem_limit_bytes=24 * 2**20
        ),
        cost_estimate=pl.CostEstimate(flops=packed * NB, bytes_accessed=8 * packed * NB, transcendentals=0),
        name="spread",
    )(part_sum)


def eliminate(block):
    lane = lax.broadcasted_iota(jnp.int32, (8, NB), 1)
    sub = lax.broadcasted_iota(jnp.int32, (8, 1), 0)
    groups = [block[8 * g : 8 * g + 8, :] for g in range(NB // 8)]
    for j in range(NB - 1):
        first, r = divmod(j, 8)
        row = groups[first][r : r + 1, :]
        inverse = 1.0 / row[:, j : j + 1]
        here = lane == j
        row = jnp.where(here[:1], 1.0, row)
        for g in range(first if r < 7 else first + 1, NB // 8):
            c = groups[g]
            coef = c[:, j : j + 1] * inverse
            if g == first:
                live = sub > r
                coef = jnp.where(live, coef, 0.0)
                base = jnp.where(here & live, 0.0, c)
            else:
                base = jnp.where(here, 0.0, c)
            groups[g] = base - coef * row
    return jnp.concatenate(groups, axis=0)


def hdot(a, b, dims=((1,), (0,))):
    return lax.dot_general(
        a, b, (dims, ((), ())), precision=lax.Precision.HIGHEST, preferred_element_type=jnp.float32
    )


def factor_kernel(rows_all, g_ref, r_ref, u_ref, mh_ref, ml_ref, work):
    n = r_ref.shape[0]
    for b, (bi, bj) in enumerate(lower_blocks(n)):
        rows = slice(bi * NB, (bi + 1) * NB)
        cols = slice(bj * NB, (bj + 1) * NB)
        block = g_ref[b * NB : (b + 1) * NB, :] / rows_all
        work[rows, cols] = block
        if bi != bj:
            work[cols, rows] = block.T
    work[:, n:] = (
        lax.broadcasted_iota(jnp.int32, (n, n), 0) == lax.broadcasted_iota(jnp.int32, (n, n), 1)
    ).astype(jnp.float32)

    def step(k, carry):
        at = pl.multiple_of(k * NB, NB)
        here = pl.ds(at, NB)
        done = eliminate(work[here, here])
        i = lax.broadcasted_iota(jnp.int32, (NB, NB), 0)
        j = lax.broadcasted_iota(jnp.int32, (NB, NB), 1)
        scale = lax.rsqrt(jnp.sum(jnp.where(i == j, done, 0.0), axis=1, keepdims=True))
        inverse = jnp.where(i > j, done, jnp.where(i == j, 1.0, 0.0)) * scale
        panel = hdot(inverse, work[here, :])
        work[here, :] = panel
        work[here, here] = jnp.where(i <= j, done, 0.0) * scale
        column = lax.broadcasted_iota(jnp.int32, (NB, n), 1)
        coef = jnp.where(column >= at + NB, panel[:, :n], 0.0)

        @pl.when(k < n // NB - 1)
        def _():
            work[...] -= hdot(coef, panel, ((0,), (0,)))

        return carry

    lax.fori_loop(0, n // NB, step, 0)
    i = lax.broadcasted_iota(jnp.int32, (n, n), 0)
    j = lax.broadcasted_iota(jnp.int32, (n, n), 1)
    u_ref[...] = jnp.where(i <= j, work[:, :n], 0.0)
    m = hdot(r_ref[...], work[:, n:], ((1,), (1,)))
    h, l = split(m)
    mh_ref[...] = h
    ml_ref[...] = l


def factorise(gram, inverse_factor, rows_all):
    n = inverse_factor.shape[0]
    return pl.pallas_call(
        functools.partial(factor_kernel, rows_all),
        out_shape=[
            jax.ShapeDtypeStruct((n, n), jnp.float32),
            jax.ShapeDtypeStruct((n, n), jnp.bfloat16),
            jax.ShapeDtypeStruct((n, n), jnp.bfloat16),
        ],
        in_specs=[pl.BlockSpec(memory_space=pltpu.VMEM)] * 2,
        out_specs=[pl.BlockSpec(memory_space=pltpu.VMEM)] * 3,
        scratch_shapes=[pltpu.VMEM((n, 2 * n), jnp.float32)],
        compiler_params=pltpu.CompilerParams(vmem_limit_bytes=40 * 2**20),
        cost_estimate=pl.CostEstimate(flops=40 * n**3, bytes_accessed=16 * n * n, transcendentals=0),
        name="factorise",
    )(gram, inverse_factor)


def last_kernel(pieces, index_ref, *refs):
    mh_ref, ml_ref = refs[PER_STEP * pieces : PER_STEP * pieces + 2]
    o_ref = refs[-1]
    x = jnp.concatenate([r[0] for r in refs[: PER_STEP * pieces]], axis=0)
    a, b = upper_product(x, mh_ref[...], ml_ref[...])
    shape = (PER_STEP, o_ref.shape[1], HALF)
    o_ref[:, :, :HALF] = a.reshape(shape)
    o_ref[:, :, HALF:] = b.reshape(shape)


def last_product(index, pieces, mh, ml):
    n = mh.shape[0]
    rows = sum(x.shape[1] for x in pieces)
    whole = pl.BlockSpec((n, n), lambda i, idx: (0, 0))

    def tile(x, t):
        return pl.BlockSpec((1,) + x.shape[1:], lambda i, idx: (idx[i * PER_STEP + t], 0, 0))

    operands = [x for _ in range(PER_STEP) for x in pieces] + [mh, ml]
    specs = [tile(x, t) for t in range(PER_STEP) for x in pieces] + [whole, whole]
    return pl.pallas_call(
        functools.partial(last_kernel, len(pieces)),
        grid_spec=pltpu.PrefetchScalarGridSpec(
            num_scalar_prefetch=1,
            grid=(OWN_TILES // PER_STEP,),
            in_specs=specs,
            out_specs=pl.BlockSpec((PER_STEP, rows, n), lambda i, idx: (i, 0, 0)),
        ),
        out_shape=jax.ShapeDtypeStruct((OWN_TILES, rows, n), jnp.float32),
        compiler_params=pltpu.CompilerParams(vmem_limit_bytes=40 * 2**20),
        cost_estimate=pl.CostEstimate(
            flops=6 * OWN_TILES * rows * n * n, bytes_accessed=8 * OWN_TILES * rows * n, transcendentals=0
        ),
        name="last_product",
    )(index, *operands)


def seats(owner, count, scenes):
    capacity = owner.shape[0]
    position = jnp.arange(capacity, dtype=jnp.int32)
    is_live = position < count
    earlier = (owner[:, None] == owner[None, :]) & is_live[None, :] & (position[None, :] < position[:, None])
    rank = earlier.astype(jnp.int32).sum(1)
    return is_live, rank


def shards(observations, inverse_factor, tile_count, tile_owner, tile_slot):
    scenes = lax.axis_size("scene")
    devices = scenes * lax.axis_size("rows")
    capacity = tile_owner.shape[0]
    pair_most = capacity // scenes
    tile_rows, n = observations.shape[1:]
    position = jnp.arange(capacity, dtype=jnp.int32)

    is_live, rank = seats(tile_owner, tile_count[0], scenes)
    target = jnp.where(is_live, tile_owner * pair_most + rank, -1)
    selector = (target[None, :] == position[:, None]).astype(jnp.int32)
    chosen = (selector * position[None, :]).sum(1)

    def exchange(outgoing):
        rows = outgoing.shape[1]
        return lax.all_to_all(
            outgoing.reshape(scenes, pair_most, rows, n), "scene", split_axis=0, concat_axis=0, tiled=True
        ).reshape(capacity, rows, n)

    first, count = lax.optimization_barrier((gather_rows(chosen, observations, 0, FIRST), tile_count))
    first = exchange(first)
    rest = gather_rows(chosen, observations, FIRST, tile_rows - FIRST)

    me = lax.axis_index("scene")
    note = jnp.where(is_live, (tile_owner * pair_most + rank) * OWN_TILES + tile_slot, -1)
    note = jnp.zeros((8, 128), jnp.int32).at[0, :capacity].set(note)
    chunk = -(-len(lower_blocks(n)) * NB // devices // 8) * 8
    gram = local_gram(count, observations, inverse_factor, chunk * devices)
    rows = lax.axis_size("rows")
    part_sum, notes = sum_part(gram, note, scenes, rows)
    rest, part_sum = lax.optimization_barrier((rest, part_sum))
    rest = exchange(rest)
    gram = spread(part_sum, rows)
    notes = notes[:, 0, :capacity]
    seat = notes // OWN_TILES
    mine = (notes >= 0) & (seat // pair_most == me)
    place = jnp.arange(scenes, dtype=jnp.int32)[:, None] * pair_most + seat % pair_most
    match = mine[None] & ((notes % OWN_TILES)[None] == jnp.arange(OWN_TILES, dtype=jnp.int32)[:, None, None])
    order = jnp.where(match, place[None], 0).sum((1, 2))

    factor, mh, ml = factorise(gram, inverse_factor, devices * OWN_TILES * tile_rows)
    return last_product(order, [first, rest], mh, ml), factor


def solution(mesh):
    in_specs = (
        P(("scene", "rows"), None, None),
        P(),
        P(("scene", "rows")),
        P(("scene", "rows")),
        P(("scene", "rows")),
    )
    out_specs = (P(("scene", "rows"), None, None), P())
    return jax.shard_map(shards, mesh=mesh, in_specs=in_specs, out_specs=out_specs, check_vma=False)
```

```python
import functools

import jax
import jax.numpy as jnp
from jax import lax
from jax.experimental import pallas as pl
from jax.experimental.pallas import tpu as pltpu
from jax.sharding import PartitionSpec as P

OWN_TILES = 8
NB = 128
HALF = 256
FIRST = 64
PER_STEP = 4


def split(x):
    hi = x.astype(jnp.bfloat16)
    return hi, (x - hi.astype(jnp.float32)).astype(jnp.bfloat16)


def mm(a, b):
    return jnp.dot(a, b, preferred_element_type=jnp.float32)


def upper_product(x, uh, ul):
    xh, xl = split(x)
    left = slice(0, HALF)
    right = slice(HALF, None)
    a = mm(xh[:, left], uh[left, left]) + (mm(xh[:, left], ul[left, left]) + mm(xl[:, left], uh[left, left]))
    b = mm(xh, uh[:, right]) + (mm(xh, ul[:, right]) + mm(xl, uh[:, right]))
    return a, b


def copy_kernel(start, index_ref, x_ref, o_ref, held, in_sems, out_sems):
    count, rows = o_ref.shape[:2]

    def read(i):
        return pltpu.make_async_copy(x_ref.at[index_ref[i], pl.ds(start, rows), :], held.at[i], in_sems.at[i])

    def write(i):
        return pltpu.make_async_copy(held.at[i], o_ref.at[i], out_sems.at[i])

    for i in range(count):
        read(i).start()
    for i in range(count):
        read(i).wait()
        write(i).start()
    for i in range(count):
        write(i).wait()


def gather_rows(index, tiles, start, rows):
    shape = (index.shape[0], rows, tiles.shape[2])
    anywhere = pl.BlockSpec(memory_space=pl.ANY)
    return pl.pallas_call(
        functools.partial(copy_kernel, start),
        in_specs=[pl.BlockSpec(memory_space=pltpu.SMEM), anywhere],
        out_specs=anywhere,
        out_shape=jax.ShapeDtypeStruct(shape, tiles.dtype),
        scratch_shapes=[
            pltpu.VMEM(shape, tiles.dtype),
            pltpu.SemaphoreType.DMA((shape[0],)),
            pltpu.SemaphoreType.DMA((shape[0],)),
        ],
        compiler_params=pltpu.CompilerParams(vmem_limit_bytes=60 * 2**20),
        name="gather_rows",
    )(index, tiles)


def lower_blocks(n):
    return [(i, j) for i in range(n // NB) for j in range(i + 1)]


def gram_kernel(count_ref, x_ref, r_ref, g_ref, rh, rl, low, cross):
    i = pl.program_id(0)

    @pl.when(i == 0)
    def _():
        h, l = split(r_ref[...])
        rh[...] = h
        rl[...] = l
        low[...] = jnp.zeros_like(low)
        cross[...] = jnp.zeros_like(cross)

    @pl.when(i < count_ref[0])
    def _():
        a, b = upper_product(x_ref[0], rh[...], rl[...])
        ah, al = split(a)
        bh, bl = split(b)
        at = ah.T
        bt = bh.T
        low[:HALF, :HALF] += mm(at, ah)
        low[HALF:, :HALF] += mm(bt, ah)
        low[HALF:, HALF:] += mm(bt, bh)
        cross[:HALF, :HALF] += mm(at, al)
        cross[:HALF, HALF:] += mm(at, bl)
        cross[HALF:, :HALF] += mm(bt, al)
        cross[HALF:, HALF:] += mm(bt, bl)

    @pl.when(i == pl.num_programs(0) - 1)
    def _():
        blocks = lower_blocks(low.shape[0])
        for k, (bi, bj) in enumerate(blocks):
            rows = slice(bi * NB, (bi + 1) * NB)
            cols = slice(bj * NB, (bj + 1) * NB)
            g_ref[k * NB : (k + 1) * NB, :] = low[rows, cols] + (cross[rows, cols] + cross[cols, rows].T)
        used = len(blocks) * NB
        if used < g_ref.shape[0]:
            g_ref[used:, :] = jnp.zeros((g_ref.shape[0] - used, NB), jnp.float32)


def local_gram(count, tiles, inverse_factor, packed):
    capacity, rows, n = tiles.shape
    return pl.pallas_call(
        gram_kernel,
        grid_spec=pltpu.PrefetchScalarGridSpec(
            num_scalar_prefetch=1,
            grid=(capacity,),
            in_specs=[
                pl.BlockSpec(
                    (1, rows, n), lambda i, c: (jnp.minimum(i, jnp.maximum(c[0] - 1, 0)), 0, 0)
                ),
                pl.BlockSpec((n, n), lambda i, c: (0, 0)),
            ],
            out_specs=pl.BlockSpec((packed, NB), lambda i, c: (0, 0)),
            scratch_shapes=[
                pltpu.VMEM((n, n), jnp.bfloat16),
                pltpu.VMEM((n, n), jnp.bfloat16),
                pltpu.VMEM((n, n), jnp.float32),
                pltpu.VMEM((n, n), jnp.float32),
            ],
        ),
        out_shape=jax.ShapeDtypeStruct((packed, NB), jnp.float32),
        compiler_params=pltpu.CompilerParams(vmem_limit_bytes=60 * 2**20),
        cost_estimate=pl.CostEstimate(
            flops=8 * capacity * rows * n * n, bytes_accessed=4 * capacity * rows * n, transcendentals=0
        ),
        name="local_gram",
    )(count, tiles, inverse_factor)


def place():
    row = lax.axis_index("rows")
    return lax.axis_index("scene"), row, lax.rem(row, 2), lax.div(row, 2)


def greet(peers):
    barrier = pltpu.get_barrier_semaphore()
    for peer in peers:
        pl.semaphore_signal(barrier, inc=1, device_id=peer, device_id_type=pl.DeviceIdType.MESH)
    pl.semaphore_wait(barrier, len(peers))


def sender(ss, rs):
    used = [0]

    def send(src, dst, peer):
        k = used[0]
        used[0] += 1
        copy = pltpu.make_async_remote_copy(
            src_ref=src, dst_ref=dst, send_sem=ss.at[k], recv_sem=rs.at[k],
            device_id=peer, device_id_type=pl.DeviceIdType.MESH,
        )
        copy.start()
        return copy

    return send


def span(start, size):
    return pl.ds(pl.multiple_of(start, 8), size)


def sum_kernel(scenes, rows, g_ref, note_ref, out_ref, notes_ref, h0, h1, rx0, rx1, rx2, ss, rs):
    packed = g_ref.shape[0]
    half, part, chunk = packed // 2, packed // rows, packed // rows // scenes
    mates = rows // 2
    scene, row, core, mate = place()
    pair = (scene, row + 1 - 2 * core)
    plane = [(scene, lax.rem(mate + d, mates) * 2 + core) for d in range(1, mates)]
    line = [(lax.rem(scene + d, scenes), row) for d in range(1, scenes)]
    greet([pair] + plane + line)
    send = sender(ss, rs)

    copy = send(g_ref.at[span((1 - core) * half, half)], rx0, pair)
    copy.wait()
    h0[...] = g_ref[span(core * half, half), :] + rx0[...]

    copies = [send(h0.at[span(lax.div(p[1], 2) * part, part)], rx1.at[d], p) for d, p in enumerate(plane)]
    total = h0[span(mate * part, part), :]
    for d, copy in enumerate(copies):
        copy.wait()
        total += rx1[d]
    h1[...] = total

    copies = [send(h1.at[span(p[0] * chunk, chunk)], rx2.at[d], p) for d, p in enumerate(line)]
    notes = [send(note_ref, notes_ref.at[scene], p) for p in line]
    notes_ref[scene] = note_ref[...]
    total = h1[span(scene * chunk, chunk), :]
    for d, copy in enumerate(copies):
        copy.wait()
        total += rx2[d]

    own = span(scene * chunk, chunk)
    out_ref[own, :] = total
    for copy in [send(out_ref.at[own], out_ref.at[own], p) for p in line] + notes:
        copy.wait()


def sum_part(gram, note, scenes, rows):
    packed = gram.shape[0]
    half, part, chunk = packed // 2, packed // rows, packed // rows // scenes
    copies = rows // 2 + 3 * (scenes - 1)
    whole = pl.BlockSpec(memory_space=pltpu.VMEM)
    return pl.pallas_call(
        functools.partial(sum_kernel, scenes, rows),
        out_shape=[
            jax.ShapeDtypeStruct((part, NB), gram.dtype),
            jax.ShapeDtypeStruct((scenes,) + note.shape, note.dtype),
        ],
        in_specs=[whole, whole],
        out_specs=[whole, whole],
        scratch_shapes=[
            pltpu.VMEM((half, NB), jnp.float32),
            pltpu.VMEM((part, NB), jnp.float32),
            pltpu.VMEM((half, NB), jnp.float32),
            pltpu.VMEM((rows // 2 - 1, part, NB), jnp.float32),
            pltpu.VMEM((scenes - 1, chunk, NB), jnp.float32),
            pltpu.SemaphoreType.DMA((copies,)),
            pltpu.SemaphoreType.DMA((copies,)),
        ],
        compiler_params=pltpu.CompilerParams(
            collective_id=0, has_side_effects=True, vmem_limit_bytes=24 * 2**20
        ),
        cost_estimate=pl.CostEstimate(flops=10 * packed * NB, bytes_accessed=16 * packed * NB, transcendentals=0),
        name="sum_part",
    )(gram, note)


def spread_kernel(rows, h_ref, out_ref, ss, rs):
    packed = out_ref.shape[0]
    half, part = packed // 2, packed // rows
    mates = rows // 2
    scene, row, core, mate = place()
    pair = (scene, row + 1 - 2 * core)
    plane = [(scene, lax.rem(mate + d, mates) * 2 + core) for d in range(1, mates)]
    greet([pair] + plane)
    send = sender(ss, rs)
    own = span(core * half + mate * part, part)
    copies = [send(h_ref, out_ref.at[own], p) for p in plane]
    out_ref[own, :] = h_ref[...]
    for copy in copies:
        copy.wait()
    own = span(core * half, half)
    send(out_ref.at[own], out_ref.at[own], pair).wait()


def spread(part_sum, rows):
    whole = pl.BlockSpec(memory_space=pltpu.VMEM)
    packed = part_sum.shape[0] * rows
    return pl.pallas_call(
        functools.partial(spread_kernel, rows),
        out_shape=jax.ShapeDtypeStruct((packed, NB), part_sum.dtype),
        in_specs=[whole],
        out_specs=whole,
        scratch_shapes=[pltpu.SemaphoreType.DMA((rows // 2,)), pltpu.SemaphoreType.DMA((rows // 2,))],
        compiler_params=pltpu.CompilerParams(
            collective_id=1, has_side_effects=True, vmem_limit_bytes=24 * 2**20
        ),
        cost_estimate=pl.CostEstimate(flops=packed * NB, bytes_accessed=8 * packed * NB, transcendentals=0),
        name="spread",
    )(part_sum)


def eliminate(block):
    lane = lax.broadcasted_iota(jnp.int32, (8, NB), 1)
    sub = lax.broadcasted_iota(jnp.int32, (8, 1), 0)
    groups = [block[8 * g : 8 * g + 8, :] for g in range(NB // 8)]
    for j in range(NB - 1):
        first, r = divmod(j, 8)
        row = groups[first][r : r + 1, :]
        inverse = 1.0 / row[:, j : j + 1]
        here = lane == j
        row = jnp.where(here[:1], 1.0, row)
        for g in range(first if r < 7 else first + 1, NB // 8):
            c = groups[g]
            coef = c[:, j : j + 1] * inverse
            if g == first:
                live = sub > r
                coef = jnp.where(live, coef, 0.0)
                base = jnp.where(here & live, 0.0, c)
            else:
                base = jnp.where(here, 0.0, c)
            groups[g] = base - coef * row
    return jnp.concatenate(groups, axis=0)


def hdot(a, b, dims=((1,), (0,))):
    return lax.dot_general(
        a, b, (dims, ((), ())), precision=lax.Precision.HIGHEST, preferred_element_type=jnp.float32
    )


def factor_kernel(rows_all, g_ref, r_ref, u_ref, mh_ref, ml_ref, work):
    n = r_ref.shape[0]
    for b, (bi, bj) in enumerate(lower_blocks(n)):
        rows = slice(bi * NB, (bi + 1) * NB)
        cols = slice(bj * NB, (bj + 1) * NB)
        block = g_ref[b * NB : (b + 1) * NB, :] / rows_all
        work[rows, cols] = block
        if bi != bj:
            work[cols, rows] = block.T
    work[:, n:] = (
        lax.broadcasted_iota(jnp.int32, (n, n), 0) == lax.broadcasted_iota(jnp.int32, (n, n), 1)
    ).astype(jnp.float32)

    def step(k, carry):
        at = pl.multiple_of(k * NB, NB)
        here = pl.ds(at, NB)
        done = eliminate(work[here, here])
        i = lax.broadcasted_iota(jnp.int32, (NB, NB), 0)
        j = lax.broadcasted_iota(jnp.int32, (NB, NB), 1)
        scale = lax.rsqrt(jnp.sum(jnp.where(i == j, done, 0.0), axis=1, keepdims=True))
        inverse = jnp.where(i > j, done, jnp.where(i == j, 1.0, 0.0)) * scale
        panel = hdot(inverse, work[here, :])
        work[here, :] = panel
        work[here, here] = jnp.where(i <= j, done, 0.0) * scale
        column = lax.broadcasted_iota(jnp.int32, (NB, n), 1)
        coef = jnp.where(column >= at + NB, panel[:, :n], 0.0)

        @pl.when(k < n // NB - 1)
        def _():
            work[...] -= hdot(coef, panel, ((0,), (0,)))

        return carry

    lax.fori_loop(0, n // NB, step, 0)
    i = lax.broadcasted_iota(jnp.int32, (n, n), 0)
    j = lax.broadcasted_iota(jnp.int32, (n, n), 1)
    u_ref[...] = jnp.where(i <= j, work[:, :n], 0.0)
    m = hdot(r_ref[...], work[:, n:], ((1,), (1,)))
    h, l = split(m)
    mh_ref[...] = h
    ml_ref[...] = l


def factorise(gram, inverse_factor, rows_all):
    n = inverse_factor.shape[0]
    return pl.pallas_call(
        functools.partial(factor_kernel, rows_all),
        out_shape=[
            jax.ShapeDtypeStruct((n, n), jnp.float32),
            jax.ShapeDtypeStruct((n, n), jnp.bfloat16),
            jax.ShapeDtypeStruct((n, n), jnp.bfloat16),
        ],
        in_specs=[pl.BlockSpec(memory_space=pltpu.VMEM)] * 2,
        out_specs=[pl.BlockSpec(memory_space=pltpu.VMEM)] * 3,
        scratch_shapes=[pltpu.VMEM((n, 2 * n), jnp.float32)],
        compiler_params=pltpu.CompilerParams(vmem_limit_bytes=40 * 2**20),
        cost_estimate=pl.CostEstimate(flops=40 * n**3, bytes_accessed=16 * n * n, transcendentals=0),
        name="factorise",
    )(gram, inverse_factor)


def last_kernel(pieces, index_ref, *refs):
    mh_ref, ml_ref = refs[PER_STEP * pieces : PER_STEP * pieces + 2]
    o_ref = refs[-1]
    x = jnp.concatenate([r[0] for r in refs[: PER_STEP * pieces]], axis=0)
    a, b = upper_product(x, mh_ref[...], ml_ref[...])
    shape = (PER_STEP, o_ref.shape[1], HALF)
    o_ref[:, :, :HALF] = a.reshape(shape)
    o_ref[:, :, HALF:] = b.reshape(shape)


def last_product(index, pieces, mh, ml):
    n = mh.shape[0]
    rows = sum(x.shape[1] for x in pieces)
    whole = pl.BlockSpec((n, n), lambda i, idx: (0, 0))

    def tile(x, t):
        return pl.BlockSpec((1,) + x.shape[1:], lambda i, idx: (idx[i * PER_STEP + t], 0, 0))

    operands = [x for _ in range(PER_STEP) for x in pieces] + [mh, ml]
    specs = [tile(x, t) for t in range(PER_STEP) for x in pieces] + [whole, whole]
    return pl.pallas_call(
        functools.partial(last_kernel, len(pieces)),
        grid_spec=pltpu.PrefetchScalarGridSpec(
            num_scalar_prefetch=1,
            grid=(OWN_TILES // PER_STEP,),
            in_specs=specs,
            out_specs=pl.BlockSpec((PER_STEP, rows, n), lambda i, idx: (i, 0, 0)),
        ),
        out_shape=jax.ShapeDtypeStruct((OWN_TILES, rows, n), jnp.float32),
        compiler_params=pltpu.CompilerParams(vmem_limit_bytes=40 * 2**20),
        cost_estimate=pl.CostEstimate(
            flops=6 * OWN_TILES * rows * n * n, bytes_accessed=8 * OWN_TILES * rows * n, transcendentals=0
        ),
        name="last_product",
    )(index, *operands)


def seats(owner, count, scenes):
    capacity = owner.shape[0]
    position = jnp.arange(capacity, dtype=jnp.int32)
    is_live = position < count
    earlier = (owner[:, None] == owner[None, :]) & is_live[None, :] & (position[None, :] < position[:, None])
    rank = earlier.astype(jnp.int32).sum(1)
    return is_live, rank


def shards(observations, inverse_factor, tile_count, tile_owner, tile_slot):
    scenes = lax.axis_size("scene")
    devices = scenes * lax.axis_size("rows")
    capacity = tile_owner.shape[0]
    pair_most = capacity // scenes
    tile_rows, n = observations.shape[1:]
    position = jnp.arange(capacity, dtype=jnp.int32)

    is_live, rank = seats(tile_owner, tile_count[0], scenes)
    target = jnp.where(is_live, tile_owner * pair_most + rank, -1)
    selector = (target[None, :] == position[:, None]).astype(jnp.int32)
    chosen = (selector * position[None, :]).sum(1)

    def exchange(outgoing):
        rows = outgoing.shape[1]
        return lax.all_to_all(
            outgoing.reshape(scenes, pair_most, rows, n), "scene", split_axis=0, concat_axis=0, tiled=True
        ).reshape(capacity, rows, n)

    first, count = lax.optimization_barrier((gather_rows(chosen, observations, 0, FIRST), tile_count))
    first = exchange(first)
    rest = gather_rows(chosen, observations, FIRST, tile_rows - FIRST)

    me = lax.axis_index("scene")
    note = jnp.where(is_live, (tile_owner * pair_most + rank) * OWN_TILES + tile_slot, -1)
    note = jnp.zeros((8, 128), jnp.int32).at[0, :capacity].set(note)
    chunk = -(-len(lower_blocks(n)) * NB // devices // 8) * 8
    gram = local_gram(count, observations, inverse_factor, chunk * devices)
    rows = lax.axis_size("rows")
    part_sum, notes = sum_part(gram, note, scenes, rows)
    rest, part_sum = lax.optimization_barrier((rest, part_sum))
    rest = exchange(rest)
    gram = spread(part_sum, rows)
    notes = notes[:, 0, :capacity]
    seat = notes // OWN_TILES
    mine = (notes >= 0) & (seat // pair_most == me)
    place = jnp.arange(scenes, dtype=jnp.int32)[:, None] * pair_most + seat % pair_most
    match = mine[None] & ((notes % OWN_TILES)[None] == jnp.arange(OWN_TILES, dtype=jnp.int32)[:, None, None])
    order = jnp.where(match, place[None], 0).sum((1, 2))

    factor, mh, ml = factorise(gram, inverse_factor, devices * OWN_TILES * tile_rows)
    return last_product(order, [first, rest], mh, ml), factor


def solution(mesh):
    in_specs = (
        P(("scene", "rows"), None, None),
        P(),
        P(("scene", "rows")),
        P(("scene", "rows")),
        P(("scene", "rows")),
    )
    out_specs = (P(("scene", "rows"), None, None), P())
    return jax.shard_map(shards, mesh=mesh, in_specs=in_specs, out_specs=out_specs, check_vma=False)
```

```python
import functools

import jax
import jax.numpy as jnp
from jax import lax
from jax.experimental import pallas as pl
from jax.experimental.pallas import tpu as pltpu
from jax.sharding import PartitionSpec as P

OWN_TILES = 8
NB = 128
HALF = 256
FIRST = 48
PER_STEP = 4


def split(x):
    hi = x.astype(jnp.bfloat16)
    return hi, (x - hi.astype(jnp.float32)).astype(jnp.bfloat16)


def mm(a, b):
    return jnp.dot(a, b, preferred_element_type=jnp.float32)


def upper_product(x, uh, ul):
    xh, xl = split(x)
    left = slice(0, HALF)
    right = slice(HALF, None)
    a = mm(xh[:, left], uh[left, left]) + (mm(xh[:, left], ul[left, left]) + mm(xl[:, left], uh[left, left]))
    b = mm(xh, uh[:, right]) + (mm(xh, ul[:, right]) + mm(xl, uh[:, right]))
    return a, b


def copy_kernel(start, index_ref, x_ref, o_ref, held, in_sems, out_sems):
    count, rows = o_ref.shape[:2]

    def read(i):
        return pltpu.make_async_copy(x_ref.at[index_ref[i], pl.ds(start, rows), :], held.at[i], in_sems.at[i])

    def write(i):
        return pltpu.make_async_copy(held.at[i], o_ref.at[i], out_sems.at[i])

    for i in range(count):
        read(i).start()
    for i in range(count):
        read(i).wait()
        write(i).start()
    for i in range(count):
        write(i).wait()


def gather_rows(index, tiles, start, rows):
    shape = (index.shape[0], rows, tiles.shape[2])
    anywhere = pl.BlockSpec(memory_space=pl.ANY)
    return pl.pallas_call(
        functools.partial(copy_kernel, start),
        in_specs=[pl.BlockSpec(memory_space=pltpu.SMEM), anywhere],
        out_specs=anywhere,
        out_shape=jax.ShapeDtypeStruct(shape, tiles.dtype),
        scratch_shapes=[
            pltpu.VMEM(shape, tiles.dtype),
            pltpu.SemaphoreType.DMA((shape[0],)),
            pltpu.SemaphoreType.DMA((shape[0],)),
        ],
        compiler_params=pltpu.CompilerParams(vmem_limit_bytes=60 * 2**20),
        name="gather_rows",
    )(index, tiles)


def lower_blocks(n):
    return [(i, j) for i in range(n // NB) for j in range(i + 1)]


def gram_kernel(count_ref, x_ref, r_ref, g_ref, rh, rl, low, cross):
    i = pl.program_id(0)

    @pl.when(i == 0)
    def _():
        h, l = split(r_ref[...])
        rh[...] = h
        rl[...] = l
        low[...] = jnp.zeros_like(low)
        cross[...] = jnp.zeros_like(cross)

    @pl.when(i < count_ref[0])
    def _():
        a, b = upper_product(x_ref[0], rh[...], rl[...])
        ah, al = split(a)
        bh, bl = split(b)
        at = ah.T
        bt = bh.T
        low[:HALF, :HALF] += mm(at, ah)
        low[HALF:, :HALF] += mm(bt, ah)
        low[HALF:, HALF:] += mm(bt, bh)
        cross[:HALF, :HALF] += mm(at, al)
        cross[:HALF, HALF:] += mm(at, bl)
        cross[HALF:, :HALF] += mm(bt, al)
        cross[HALF:, HALF:] += mm(bt, bl)

    @pl.when(i == pl.num_programs(0) - 1)
    def _():
        blocks = lower_blocks(low.shape[0])
        for k, (bi, bj) in enumerate(blocks):
            rows = slice(bi * NB, (bi + 1) * NB)
            cols = slice(bj * NB, (bj + 1) * NB)
            g_ref[k * NB : (k + 1) * NB, :] = low[rows, cols] + (cross[rows, cols] + cross[cols, rows].T)
        used = len(blocks) * NB
        if used < g_ref.shape[0]:
            g_ref[used:, :] = jnp.zeros((g_ref.shape[0] - used, NB), jnp.float32)


def local_gram(count, tiles, inverse_factor, packed):
    capacity, rows, n = tiles.shape
    return pl.pallas_call(
        gram_kernel,
        grid_spec=pltpu.PrefetchScalarGridSpec(
            num_scalar_prefetch=1,
            grid=(capacity,),
            in_specs=[
                pl.BlockSpec(
                    (1, rows, n), lambda i, c: (jnp.minimum(i, jnp.maximum(c[0] - 1, 0)), 0, 0)
                ),
                pl.BlockSpec((n, n), lambda i, c: (0, 0)),
            ],
            out_specs=pl.BlockSpec((packed, NB), lambda i, c: (0, 0)),
            scratch_shapes=[
                pltpu.VMEM((n, n), jnp.bfloat16),
                pltpu.VMEM((n, n), jnp.bfloat16),
                pltpu.VMEM((n, n), jnp.float32),
                pltpu.VMEM((n, n), jnp.float32),
            ],
        ),
        out_shape=jax.ShapeDtypeStruct((packed, NB), jnp.float32),
        compiler_params=pltpu.CompilerParams(vmem_limit_bytes=60 * 2**20),
        cost_estimate=pl.CostEstimate(
            flops=8 * capacity * rows * n * n, bytes_accessed=4 * capacity * rows * n, transcendentals=0
        ),
        name="local_gram",
    )(count, tiles, inverse_factor)


def place():
    row = lax.axis_index("rows")
    return lax.axis_index("scene"), row, lax.rem(row, 2), lax.div(row, 2)


def greet(peers):
    barrier = pltpu.get_barrier_semaphore()
    for peer in peers:
        pl.semaphore_signal(barrier, inc=1, device_id=peer, device_id_type=pl.DeviceIdType.MESH)
    pl.semaphore_wait(barrier, len(peers))


def sender(ss, rs):
    used = [0]

    def send(src, dst, peer):
        k = used[0]
        used[0] += 1
        copy = pltpu.make_async_remote_copy(
            src_ref=src, dst_ref=dst, send_sem=ss.at[k], recv_sem=rs.at[k],
            device_id=peer, device_id_type=pl.DeviceIdType.MESH,
        )
        copy.start()
        return copy

    return send


def span(start, size):
    return pl.ds(pl.multiple_of(start, 8), size)


def eliminate(block):
    lane = lax.broadcasted_iota(jnp.int32, (8, NB), 1)
    sub = lax.broadcasted_iota(jnp.int32, (8, 1), 0)
    groups = [block[8 * g : 8 * g + 8, :] for g in range(NB // 8)]
    for j in range(NB - 1):
        first, r = divmod(j, 8)
        row = groups[first][r : r + 1, :]
        inverse = 1.0 / row[:, j : j + 1]
        here = lane == j
        row = jnp.where(here[:1], 1.0, row)
        for g in range(first if r < 7 else first + 1, NB // 8):
            c = groups[g]
            coef = c[:, j : j + 1] * inverse
            if g == first:
                live = sub > r
                coef = jnp.where(live, coef, 0.0)
                base = jnp.where(here & live, 0.0, c)
            else:
                base = jnp.where(here, 0.0, c)
            groups[g] = base - coef * row
    return jnp.concatenate(groups, axis=0)


def hdot(a, b, dims=((1,), (0,))):
    return lax.dot_general(
        a, b, (dims, ((), ())), precision=lax.Precision.HIGHEST, preferred_element_type=jnp.float32
    )


def factor_kernel(rows_all, g_ref, r_ref, u_ref, mh_ref, ml_ref, work):
    n = r_ref.shape[0]
    for b, (bi, bj) in enumerate(lower_blocks(n)):
        rows = slice(bi * NB, (bi + 1) * NB)
        cols = slice(bj * NB, (bj + 1) * NB)
        block = g_ref[b * NB : (b + 1) * NB, :] / rows_all
        work[rows, cols] = block
        if bi != bj:
            work[cols, rows] = block.T
    work[:, n:] = (
        lax.broadcasted_iota(jnp.int32, (n, n), 0) == lax.broadcasted_iota(jnp.int32, (n, n), 1)
    ).astype(jnp.float32)

    def step(k, carry):
        at = pl.multiple_of(k * NB, NB)
        here = pl.ds(at, NB)
        done = eliminate(work[here, here])
        i = lax.broadcasted_iota(jnp.int32, (NB, NB), 0)
        j = lax.broadcasted_iota(jnp.int32, (NB, NB), 1)
        scale = lax.rsqrt(jnp.sum(jnp.where(i == j, done, 0.0), axis=1, keepdims=True))
        inverse = jnp.where(i > j, done, jnp.where(i == j, 1.0, 0.0)) * scale
        panel = hdot(inverse, work[here, :])
        work[here, :] = panel
        work[here, here] = jnp.where(i <= j, done, 0.0) * scale
        column = lax.broadcasted_iota(jnp.int32, (NB, n), 1)
        coef = jnp.where(column >= at + NB, panel[:, :n], 0.0)

        @pl.when(k < n // NB - 1)
        def _():
            work[...] -= hdot(coef, panel, ((0,), (0,)))

        return carry

    lax.fori_loop(0, n // NB, step, 0)
    i = lax.broadcasted_iota(jnp.int32, (n, n), 0)
    j = lax.broadcasted_iota(jnp.int32, (n, n), 1)
    u_ref[...] = jnp.where(i <= j, work[:, :n], 0.0)
    m = hdot(r_ref[...], work[:, n:], ((1,), (1,)))
    h, l = split(m)
    mh_ref[...] = h
    ml_ref[...] = l


def heart_kernel(
    scenes, rows, rows_all, g_ref, note_ref, r_ref, rest_ref,
    u_ref, mh_ref, ml_ref, notes_ref, received_ref,
    h0, h1, rx0, rx1, rx2, part_sum, gram, work, kept, ss, rs, ls,
):
    packed = g_ref.shape[0]
    half, part, chunk = packed // 2, packed // rows, packed // rows // scenes
    mates = rows // 2
    pair_most = rest_ref.shape[0] // scenes
    scene, row, core, mate = place()
    pair = (scene, row + 1 - 2 * core)
    plane = [(scene, lax.rem(mate + d, mates) * 2 + core) for d in range(1, mates)]
    line = [(lax.rem(scene + d, scenes), row) for d in range(1, scenes)]
    greet([pair] + plane + line)
    send = sender(ss, rs)
    seat = pl.ds(scene * pair_most, pair_most)
    own_in = pltpu.make_async_copy(rest_ref.at[seat], kept, ls.at[0])
    own_out = pltpu.make_async_copy(kept, received_ref.at[seat], ls.at[1])
    own_in.start()

    copy = send(g_ref.at[span((1 - core) * half, half)], rx0, pair)
    copy.wait()
    h0[...] = g_ref[span(core * half, half), :] + rx0[...]

    copies = [send(h0.at[span(lax.div(p[1], 2) * part, part)], rx1.at[d], p) for d, p in enumerate(plane)]
    total = h0[span(mate * part, part), :]
    for d, copy in enumerate(copies):
        copy.wait()
        total += rx1[d]
    h1[...] = total

    copies = [send(h1.at[span(p[0] * chunk, chunk)], rx2.at[d], p) for d, p in enumerate(line)]
    notes = [send(note_ref, notes_ref.at[scene], p) for p in line]
    notes_ref[scene] = note_ref[...]
    total = h1[span(scene * chunk, chunk), :]
    for d, copy in enumerate(copies):
        copy.wait()
        total += rx2[d]
    own = span(scene * chunk, chunk)
    part_sum[own, :] = total
    copies = [send(part_sum.at[own], part_sum.at[own], p) for p in line] + notes

    exchange = []
    for m in range(scenes - 1, 0, -1):
        other = 0
        for bit in range(scenes.bit_length() - 1):
            have = lax.rem(lax.div(scene, 2**bit), 2)
            other += 2**bit * (1 - have if m >> bit & 1 else have)
        exchange.append(send(rest_ref.at[pl.ds(other * pair_most, pair_most)], received_ref.at[seat], (other, row)))
    for copy in copies:
        copy.wait()

    own = span(core * half + mate * part, part)
    copies = [send(part_sum, gram.at[own], p) for p in plane]
    gram[own, :] = part_sum[...]
    for copy in copies:
        copy.wait()
    own = span(core * half, half)
    send(gram.at[own], gram.at[own], pair).wait()
    own_in.wait()
    own_out.start()

    factor_kernel(rows_all, gram, r_ref, u_ref, mh_ref, ml_ref, work)
    own_out.wait()
    for copy in exchange:
        copy.wait()


def heart(gram, note, inverse_factor, rest, scenes, rows, rows_all):
    packed = gram.shape[0]
    n = inverse_factor.shape[0]
    half, part, chunk = packed // 2, packed // rows, packed // rows // scenes
    copies = rows + 4 * (scenes - 1)
    whole = pl.BlockSpec(memory_space=pltpu.VMEM)
    anywhere = pl.BlockSpec(memory_space=pl.ANY)
    return pl.pallas_call(
        functools.partial(heart_kernel, scenes, rows, rows_all),
        out_shape=[
            jax.ShapeDtypeStruct((n, n), jnp.float32),
            jax.ShapeDtypeStruct((n, n), jnp.bfloat16),
            jax.ShapeDtypeStruct((n, n), jnp.bfloat16),
            jax.ShapeDtypeStruct((scenes,) + note.shape, note.dtype),
            jax.ShapeDtypeStruct(rest.shape, rest.dtype),
        ],
        in_specs=[whole, whole, whole, anywhere],
        out_specs=[whole, whole, whole, whole, anywhere],
        scratch_shapes=[
            pltpu.VMEM((half, NB), jnp.float32),
            pltpu.VMEM((part, NB), jnp.float32),
            pltpu.VMEM((half, NB), jnp.float32),
            pltpu.VMEM((rows // 2 - 1, part, NB), jnp.float32),
            pltpu.VMEM((scenes - 1, chunk, NB), jnp.float32),
            pltpu.VMEM((part, NB), jnp.float32),
            pltpu.VMEM((packed, NB), jnp.float32),
            pltpu.VMEM((n, 2 * n), jnp.float32),
            pltpu.VMEM((rest.shape[0] // scenes,) + rest.shape[1:], jnp.float32),
            pltpu.SemaphoreType.DMA((copies,)),
            pltpu.SemaphoreType.DMA((copies,)),
            pltpu.SemaphoreType.DMA((2,)),
        ],
        compiler_params=pltpu.CompilerParams(
            collective_id=0, has_side_effects=True, vmem_limit_bytes=60 * 2**20
        ),
        name="heart",
    )(gram, note, inverse_factor, rest)


def last_kernel(pieces, index_ref, *refs):
    mh_ref, ml_ref = refs[PER_STEP * pieces : PER_STEP * pieces + 2]
    o_ref = refs[-1]
    x = jnp.concatenate([r[0] for r in refs[: PER_STEP * pieces]], axis=0)
    a, b = upper_product(x, mh_ref[...], ml_ref[...])
    shape = (PER_STEP, o_ref.shape[1], HALF)
    o_ref[:, :, :HALF] = a.reshape(shape)
    o_ref[:, :, HALF:] = b.reshape(shape)


def last_product(index, pieces, mh, ml):
    n = mh.shape[0]
    rows = sum(x.shape[1] for x in pieces)
    whole = pl.BlockSpec((n, n), lambda i, idx: (0, 0))

    def tile(x, t):
        return pl.BlockSpec((1,) + x.shape[1:], lambda i, idx: (idx[i * PER_STEP + t], 0, 0))

    operands = [x for _ in range(PER_STEP) for x in pieces] + [mh, ml]
    specs = [tile(x, t) for t in range(PER_STEP) for x in pieces] + [whole, whole]
    return pl.pallas_call(
        functools.partial(last_kernel, len(pieces)),
        grid_spec=pltpu.PrefetchScalarGridSpec(
            num_scalar_prefetch=1,
            grid=(OWN_TILES // PER_STEP,),
            in_specs=specs,
            out_specs=pl.BlockSpec((PER_STEP, rows, n), lambda i, idx: (i, 0, 0)),
        ),
        out_shape=jax.ShapeDtypeStruct((OWN_TILES, rows, n), jnp.float32),
        compiler_params=pltpu.CompilerParams(vmem_limit_bytes=40 * 2**20),
        cost_estimate=pl.CostEstimate(
            flops=6 * OWN_TILES * rows * n * n, bytes_accessed=8 * OWN_TILES * rows * n, transcendentals=0
        ),
        name="last_product",
    )(index, *operands)


def seats(owner, count, scenes):
    capacity = owner.shape[0]
    position = jnp.arange(capacity, dtype=jnp.int32)
    is_live = position < count
    earlier = (owner[:, None] == owner[None, :]) & is_live[None, :] & (position[None, :] < position[:, None])
    rank = earlier.astype(jnp.int32).sum(1)
    return is_live, rank


def shards(observations, inverse_factor, tile_count, tile_owner, tile_slot):
    scenes = lax.axis_size("scene")
    devices = scenes * lax.axis_size("rows")
    capacity = tile_owner.shape[0]
    pair_most = capacity // scenes
    tile_rows, n = observations.shape[1:]
    position = jnp.arange(capacity, dtype=jnp.int32)

    is_live, rank = seats(tile_owner, tile_count[0], scenes)
    target = jnp.where(is_live, tile_owner * pair_most + rank, -1)
    selector = (target[None, :] == position[:, None]).astype(jnp.int32)
    chosen = (selector * position[None, :]).sum(1)

    def exchange(outgoing):
        rows = outgoing.shape[1]
        return lax.all_to_all(
            outgoing.reshape(scenes, pair_most, rows, n), "scene", split_axis=0, concat_axis=0, tiled=True
        ).reshape(capacity, rows, n)

    first, count = lax.optimization_barrier((gather_rows(chosen, observations, 0, FIRST), tile_count))
    first = exchange(first)
    rest = gather_rows(chosen, observations, FIRST, tile_rows - FIRST)

    me = lax.axis_index("scene")
    note = jnp.where(is_live, (tile_owner * pair_most + rank) * OWN_TILES + tile_slot, -1)
    note = jnp.zeros((8, 128), jnp.int32).at[0, :capacity].set(note)
    chunk = -(-len(lower_blocks(n)) * NB // devices // 8) * 8
    gram = local_gram(count, observations, inverse_factor, chunk * devices)
    rows = lax.axis_size("rows")
    factor, mh, ml, notes, rest = heart(
        gram, note, inverse_factor, rest, scenes, rows, devices * OWN_TILES * tile_rows
    )
    notes = notes[:, 0, :capacity]
    seat = notes // OWN_TILES
    mine = (notes >= 0) & (seat // pair_most == me)
    place = jnp.arange(scenes, dtype=jnp.int32)[:, None] * pair_most + seat % pair_most
    match = mine[None] & ((notes % OWN_TILES)[None] == jnp.arange(OWN_TILES, dtype=jnp.int32)[:, None, None])
    order = jnp.where(match, place[None], 0).sum((1, 2))

    return last_product(order, [first, rest], mh, ml), factor


def solution(mesh):
    in_specs = (
        P(("scene", "rows"), None, None),
        P(),
        P(("scene", "rows")),
        P(("scene", "rows")),
        P(("scene", "rows")),
    )
    out_specs = (P(("scene", "rows"), None, None), P())
    return jax.shard_map(shards, mesh=mesh, in_specs=in_specs, out_specs=out_specs, check_vma=False)
```

```python
import functools

import jax
import jax.numpy as jnp
from jax import lax
from jax.experimental import pallas as pl
from jax.experimental.pallas import tpu as pltpu
from jax.sharding import PartitionSpec as P

OWN_TILES = 8
NB = 128
HALF = 256
FIRST = 64
PER_STEP = 4


def split(x):
    hi = x.astype(jnp.bfloat16)
    return hi, (x - hi.astype(jnp.float32)).astype(jnp.bfloat16)


def mm(a, b):
    return jnp.dot(a, b, preferred_element_type=jnp.float32)


def upper_product(x, uh, ul):
    xh, xl = split(x)
    left = slice(0, HALF)
    right = slice(HALF, None)
    a = mm(xh[:, left], uh[left, left]) + (mm(xh[:, left], ul[left, left]) + mm(xl[:, left], uh[left, left]))
    b = mm(xh, uh[:, right]) + (mm(xh, ul[:, right]) + mm(xl, uh[:, right]))
    return a, b


def copy_kernel(start, index_ref, x_ref, o_ref, held, in_sems, out_sems):
    count, rows = o_ref.shape[:2]

    def read(i):
        return pltpu.make_async_copy(x_ref.at[index_ref[i], pl.ds(start, rows), :], held.at[i], in_sems.at[i])

    def write(i):
        return pltpu.make_async_copy(held.at[i], o_ref.at[i], out_sems.at[i])

    for i in range(count):
        read(i).start()
    for i in range(count):
        read(i).wait()
        write(i).start()
    for i in range(count):
        write(i).wait()


def gather_rows(index, tiles, start, rows):
    shape = (index.shape[0], rows, tiles.shape[2])
    anywhere = pl.BlockSpec(memory_space=pl.ANY)
    return pl.pallas_call(
        functools.partial(copy_kernel, start),
        in_specs=[pl.BlockSpec(memory_space=pltpu.SMEM), anywhere],
        out_specs=anywhere,
        out_shape=jax.ShapeDtypeStruct(shape, tiles.dtype),
        scratch_shapes=[
            pltpu.VMEM(shape, tiles.dtype),
            pltpu.SemaphoreType.DMA((shape[0],)),
            pltpu.SemaphoreType.DMA((shape[0],)),
        ],
        compiler_params=pltpu.CompilerParams(vmem_limit_bytes=60 * 2**20),
        name="gather_rows",
    )(index, tiles)


def lower_blocks(n):
    return [(i, j) for i in range(n // NB) for j in range(i + 1)]


def gram_kernel(count_ref, x_ref, r_ref, g_ref, rh, rl, low, cross):
    i = pl.program_id(0)

    @pl.when(i == 0)
    def _():
        h, l = split(r_ref[...])
        rh[...] = h
        rl[...] = l
        low[...] = jnp.zeros_like(low)
        cross[...] = jnp.zeros_like(cross)

    @pl.when(i < count_ref[0])
    def _():
        a, b = upper_product(x_ref[0], rh[...], rl[...])
        ah, al = split(a)
        bh, bl = split(b)
        at = ah.T
        bt = bh.T
        low[:HALF, :HALF] += mm(at, ah)
        low[HALF:, :HALF] += mm(bt, ah)
        low[HALF:, HALF:] += mm(bt, bh)
        cross[:HALF, :HALF] += mm(at, al)
        cross[:HALF, HALF:] += mm(at, bl)
        cross[HALF:, :HALF] += mm(bt, al)
        cross[HALF:, HALF:] += mm(bt, bl)

    @pl.when(i == pl.num_programs(0) - 1)
    def _():
        blocks = lower_blocks(low.shape[0])
        for k, (bi, bj) in enumerate(blocks):
            rows = slice(bi * NB, (bi + 1) * NB)
            cols = slice(bj * NB, (bj + 1) * NB)
            g_ref[k * NB : (k + 1) * NB, :] = low[rows, cols] + (cross[rows, cols] + cross[cols, rows].T)
        used = len(blocks) * NB
        if used < g_ref.shape[0]:
            g_ref[used:, :] = jnp.zeros((g_ref.shape[0] - used, NB), jnp.float32)


def local_gram(count, tiles, inverse_factor, packed):
    capacity, rows, n = tiles.shape
    return pl.pallas_call(
        gram_kernel,
        grid_spec=pltpu.PrefetchScalarGridSpec(
            num_scalar_prefetch=1,
            grid=(capacity,),
            in_specs=[
                pl.BlockSpec(
                    (1, rows, n), lambda i, c: (jnp.minimum(i, jnp.maximum(c[0] - 1, 0)), 0, 0)
                ),
                pl.BlockSpec((n, n), lambda i, c: (0, 0)),
            ],
            out_specs=pl.BlockSpec((packed, NB), lambda i, c: (0, 0)),
            scratch_shapes=[
                pltpu.VMEM((n, n), jnp.bfloat16),
                pltpu.VMEM((n, n), jnp.bfloat16),
                pltpu.VMEM((n, n), jnp.float32),
                pltpu.VMEM((n, n), jnp.float32),
            ],
        ),
        out_shape=jax.ShapeDtypeStruct((packed, NB), jnp.float32),
        compiler_params=pltpu.CompilerParams(vmem_limit_bytes=60 * 2**20),
        cost_estimate=pl.CostEstimate(
            flops=8 * capacity * rows * n * n, bytes_accessed=4 * capacity * rows * n, transcendentals=0
        ),
        name="local_gram",
    )(count, tiles, inverse_factor)


def place():
    row = lax.axis_index("rows")
    return lax.axis_index("scene"), row, lax.rem(row, 2), lax.div(row, 2)


def greet(peers):
    barrier = pltpu.get_barrier_semaphore()
    for peer in peers:
        pl.semaphore_signal(barrier, inc=1, device_id=peer, device_id_type=pl.DeviceIdType.MESH)
    pl.semaphore_wait(barrier, len(peers))


def sender(ss, rs):
    used = [0]

    def send(src, dst, peer):
        k = used[0]
        used[0] += 1
        copy = pltpu.make_async_remote_copy(
            src_ref=src, dst_ref=dst, send_sem=ss.at[k], recv_sem=rs.at[k],
            device_id=peer, device_id_type=pl.DeviceIdType.MESH,
        )
        copy.start()
        return copy

    return send


def span(start, size):
    return pl.ds(pl.multiple_of(start, 8), size)


def eliminate(block):
    lane = lax.broadcasted_iota(jnp.int32, (8, NB), 1)
    sub = lax.broadcasted_iota(jnp.int32, (8, 1), 0)
    groups = [block[8 * g : 8 * g + 8, :] for g in range(NB // 8)]
    for j in range(NB - 1):
        first, r = divmod(j, 8)
        row = groups[first][r : r + 1, :]
        inverse = 1.0 / row[:, j : j + 1]
        here = lane == j
        row = jnp.where(here[:1], 1.0, row)
        for g in range(first if r < 7 else first + 1, NB // 8):
            c = groups[g]
            coef = c[:, j : j + 1] * inverse
            if g == first:
                live = sub > r
                coef = jnp.where(live, coef, 0.0)
                base = jnp.where(here & live, 0.0, c)
            else:
                base = jnp.where(here, 0.0, c)
            groups[g] = base - coef * row
    return jnp.concatenate(groups, axis=0)


def hdot(a, b, dims=((1,), (0,))):
    return lax.dot_general(
        a, b, (dims, ((), ())), precision=lax.Precision.HIGHEST, preferred_element_type=jnp.float32
    )


def factor_kernel(rows_all, g_ref, r_ref, u_ref, mh_ref, ml_ref, work):
    n = r_ref.shape[0]
    for b, (bi, bj) in enumerate(lower_blocks(n)):
        rows = slice(bi * NB, (bi + 1) * NB)
        cols = slice(bj * NB, (bj + 1) * NB)
        block = g_ref[b * NB : (b + 1) * NB, :] / rows_all
        work[rows, cols] = block
        if bi != bj:
            work[cols, rows] = block.T
    work[:, n:] = (
        lax.broadcasted_iota(jnp.int32, (n, n), 0) == lax.broadcasted_iota(jnp.int32, (n, n), 1)
    ).astype(jnp.float32)

    def step(k, carry):
        at = pl.multiple_of(k * NB, NB)
        here = pl.ds(at, NB)
        done = eliminate(work[here, here])
        i = lax.broadcasted_iota(jnp.int32, (NB, NB), 0)
        j = lax.broadcasted_iota(jnp.int32, (NB, NB), 1)
        scale = lax.rsqrt(jnp.sum(jnp.where(i == j, done, 0.0), axis=1, keepdims=True))
        inverse = jnp.where(i > j, done, jnp.where(i == j, 1.0, 0.0)) * scale
        panel = hdot(inverse, work[here, :])
        work[here, :] = panel
        work[here, here] = jnp.where(i <= j, done, 0.0) * scale
        column = lax.broadcasted_iota(jnp.int32, (NB, n), 1)
        coef = jnp.where(column >= at + NB, panel[:, :n], 0.0)

        @pl.when(k < n // NB - 1)
        def _():
            work[...] -= hdot(coef, panel, ((0,), (0,)))

        return carry

    lax.fori_loop(0, n // NB, step, 0)
    i = lax.broadcasted_iota(jnp.int32, (n, n), 0)
    j = lax.broadcasted_iota(jnp.int32, (n, n), 1)
    u_ref[...] = jnp.where(i <= j, work[:, :n], 0.0)
    m = hdot(r_ref[...], work[:, n:], ((1,), (1,)))
    h, l = split(m)
    mh_ref[...] = h
    ml_ref[...] = l


def heart_kernel(
    scenes, rows, rows_all, g_ref, note_ref, r_ref, rest_ref,
    u_ref, mh_ref, ml_ref, notes_ref, received_ref,
    h0, h1, rx0, rx1, rx2, part_sum, gram, work, kept, ss, rs, ls,
):
    packed = g_ref.shape[0]
    half, part, chunk = packed // 2, packed // rows, packed // rows // scenes
    mates = rows // 2
    pair_most = rest_ref.shape[0] // scenes
    scene, row, core, mate = place()
    pair = (scene, row + 1 - 2 * core)
    plane = [(scene, lax.rem(mate + d, mates) * 2 + core) for d in range(1, mates)]
    line = [(lax.rem(scene + d, scenes), row) for d in range(1, scenes)]
    greet([pair] + plane + line)
    send = sender(ss, rs)
    seat = pl.ds(scene * pair_most, pair_most)
    own_in = pltpu.make_async_copy(rest_ref.at[seat], kept, ls.at[0])
    own_out = pltpu.make_async_copy(kept, received_ref.at[seat], ls.at[1])
    own_in.start()

    copy = send(g_ref.at[span((1 - core) * half, half)], rx0, pair)
    copy.wait()
    h0[...] = g_ref[span(core * half, half), :] + rx0[...]

    copies = [send(h0.at[span(lax.div(p[1], 2) * part, part)], rx1.at[d], p) for d, p in enumerate(plane)]
    total = h0[span(mate * part, part), :]
    for d, copy in enumerate(copies):
        copy.wait()
        total += rx1[d]
    h1[...] = total

    copies = [send(h1.at[span(p[0] * chunk, chunk)], rx2.at[d], p) for d, p in enumerate(line)]
    notes = [send(note_ref, notes_ref.at[scene], p) for p in line]
    notes_ref[scene] = note_ref[...]
    total = h1[span(scene * chunk, chunk), :]
    for d, copy in enumerate(copies):
        copy.wait()
        total += rx2[d]
    own = span(scene * chunk, chunk)
    part_sum[own, :] = total
    copies = [send(part_sum.at[own], part_sum.at[own], p) for p in line] + notes

    exchange = []
    for m in range(scenes - 1, 0, -1):
        other = 0
        for bit in range(scenes.bit_length() - 1):
            have = lax.rem(lax.div(scene, 2**bit), 2)
            other += 2**bit * (1 - have if m >> bit & 1 else have)
        exchange.append(send(rest_ref.at[pl.ds(other * pair_most, pair_most)], received_ref.at[seat], (other, row)))
    for copy in copies:
        copy.wait()

    own = span(core * half + mate * part, part)
    copies = [send(part_sum, gram.at[own], p) for p in plane]
    gram[own, :] = part_sum[...]
    for copy in copies:
        copy.wait()
    own = span(core * half, half)
    send(gram.at[own], gram.at[own], pair).wait()
    own_in.wait()
    own_out.start()

    factor_kernel(rows_all, gram, r_ref, u_ref, mh_ref, ml_ref, work)
    own_out.wait()
    for copy in exchange:
        copy.wait()


def heart(gram, note, inverse_factor, rest, scenes, rows, rows_all):
    packed = gram.shape[0]
    n = inverse_factor.shape[0]
    half, part, chunk = packed // 2, packed // rows, packed // rows // scenes
    copies = rows + 4 * (scenes - 1)
    whole = pl.BlockSpec(memory_space=pltpu.VMEM)
    anywhere = pl.BlockSpec(memory_space=pl.ANY)
    return pl.pallas_call(
        functools.partial(heart_kernel, scenes, rows, rows_all),
        out_shape=[
            jax.ShapeDtypeStruct((n, n), jnp.float32),
            jax.ShapeDtypeStruct((n, n), jnp.bfloat16),
            jax.ShapeDtypeStruct((n, n), jnp.bfloat16),
            jax.ShapeDtypeStruct((scenes,) + note.shape, note.dtype),
            jax.ShapeDtypeStruct(rest.shape, rest.dtype),
        ],
        in_specs=[whole, whole, whole, anywhere],
        out_specs=[whole, whole, whole, whole, anywhere],
        scratch_shapes=[
            pltpu.VMEM((half, NB), jnp.float32),
            pltpu.VMEM((part, NB), jnp.float32),
            pltpu.VMEM((half, NB), jnp.float32),
            pltpu.VMEM((rows // 2 - 1, part, NB), jnp.float32),
            pltpu.VMEM((scenes - 1, chunk, NB), jnp.float32),
            pltpu.VMEM((part, NB), jnp.float32),
            pltpu.VMEM((packed, NB), jnp.float32),
            pltpu.VMEM((n, 2 * n), jnp.float32),
            pltpu.VMEM((rest.shape[0] // scenes,) + rest.shape[1:], jnp.float32),
            pltpu.SemaphoreType.DMA((copies,)),
            pltpu.SemaphoreType.DMA((copies,)),
            pltpu.SemaphoreType.DMA((2,)),
        ],
        compiler_params=pltpu.CompilerParams(
            collective_id=0, has_side_effects=True, vmem_limit_bytes=60 * 2**20
        ),
        name="heart",
    )(gram, note, inverse_factor, rest)


def last_kernel(pieces, index_ref, *refs):
    mh_ref, ml_ref = refs[PER_STEP * pieces : PER_STEP * pieces + 2]
    o_ref = refs[-1]
    x = jnp.concatenate([r[0] for r in refs[: PER_STEP * pieces]], axis=0)
    a, b = upper_product(x, mh_ref[...], ml_ref[...])
    shape = (PER_STEP, o_ref.shape[1], HALF)
    o_ref[:, :, :HALF] = a.reshape(shape)
    o_ref[:, :, HALF:] = b.reshape(shape)


def last_product(index, pieces, mh, ml):
    n = mh.shape[0]
    rows = sum(x.shape[1] for x in pieces)
    whole = pl.BlockSpec((n, n), lambda i, idx: (0, 0))

    def tile(x, t):
        return pl.BlockSpec((1,) + x.shape[1:], lambda i, idx: (idx[i * PER_STEP + t], 0, 0))

    operands = [x for _ in range(PER_STEP) for x in pieces] + [mh, ml]
    specs = [tile(x, t) for t in range(PER_STEP) for x in pieces] + [whole, whole]
    return pl.pallas_call(
        functools.partial(last_kernel, len(pieces)),
        grid_spec=pltpu.PrefetchScalarGridSpec(
            num_scalar_prefetch=1,
            grid=(OWN_TILES // PER_STEP,),
            in_specs=specs,
            out_specs=pl.BlockSpec((PER_STEP, rows, n), lambda i, idx: (i, 0, 0)),
        ),
        out_shape=jax.ShapeDtypeStruct((OWN_TILES, rows, n), jnp.float32),
        compiler_params=pltpu.CompilerParams(vmem_limit_bytes=60 * 2**20),
        cost_estimate=pl.CostEstimate(
            flops=6 * OWN_TILES * rows * n * n, bytes_accessed=8 * OWN_TILES * rows * n, transcendentals=0
        ),
        name="last_product",
    )(index, *operands)


def seats(owner, count, scenes):
    capacity = owner.shape[0]
    position = jnp.arange(capacity, dtype=jnp.int32)
    is_live = position < count
    earlier = (owner[:, None] == owner[None, :]) & is_live[None, :] & (position[None, :] < position[:, None])
    rank = earlier.astype(jnp.int32).sum(1)
    return is_live, rank


def shards(observations, inverse_factor, tile_count, tile_owner, tile_slot):
    scenes = lax.axis_size("scene")
    devices = scenes * lax.axis_size("rows")
    capacity = tile_owner.shape[0]
    pair_most = capacity // scenes
    tile_rows, n = observations.shape[1:]
    position = jnp.arange(capacity, dtype=jnp.int32)

    is_live, rank = seats(tile_owner, tile_count[0], scenes)
    target = jnp.where(is_live, tile_owner * pair_most + rank, -1)
    selector = (target[None, :] == position[:, None]).astype(jnp.int32)
    chosen = (selector * position[None, :]).sum(1)

    def exchange(outgoing):
        rows = outgoing.shape[1]
        return lax.all_to_all(
            outgoing.reshape(scenes, pair_most, rows, n), "scene", split_axis=0, concat_axis=0, tiled=True
        ).reshape(capacity, rows, n)

    first, count = lax.optimization_barrier((gather_rows(chosen, observations, 0, FIRST), tile_count))
    first = exchange(first)
    rest = gather_rows(chosen, observations, FIRST, tile_rows - FIRST)

    me = lax.axis_index("scene")
    note = jnp.where(is_live, (tile_owner * pair_most + rank) * OWN_TILES + tile_slot, -1)
    note = jnp.zeros((8, 128), jnp.int32).at[0, :capacity].set(note)
    chunk = -(-len(lower_blocks(n)) * NB // devices // 8) * 8
    gram = local_gram(count, observations, inverse_factor, chunk * devices)
    rows = lax.axis_size("rows")
    factor, mh, ml, notes, rest = heart(
        gram, note, inverse_factor, rest, scenes, rows, devices * OWN_TILES * tile_rows
    )
    notes = notes[:, 0, :capacity]
    seat = notes // OWN_TILES
    mine = (notes >= 0) & (seat // pair_most == me)
    place = jnp.arange(scenes, dtype=jnp.int32)[:, None] * pair_most + seat % pair_most
    match = mine[None] & ((notes % OWN_TILES)[None] == jnp.arange(OWN_TILES, dtype=jnp.int32)[:, None, None])
    order = jnp.where(match, place[None], 0).sum((1, 2))

    return last_product(order, [first, rest], mh, ml), factor


def solution(mesh):
    in_specs = (
        P(("scene", "rows"), None, None),
        P(),
        P(("scene", "rows")),
        P(("scene", "rows")),
        P(("scene", "rows")),
    )
    out_specs = (P(("scene", "rows"), None, None), P())
    return jax.shard_map(shards, mesh=mesh, in_specs=in_specs, out_specs=out_specs, check_vma=False)
```
